128 devices in a mesh: row: 16 (over x_lo, y, core), col: 8 (over z, x_hi).
Axes of the slice: x: 4 (x_hi: 2, x_lo: 2; x = x_hi * 2 + x_lo), y: 4, z: 4, core: 2. Of those that a mesh axis runs over, the one named last changes fastest.
Arguments:
- pair_map: float32 [1024, 1024, 128], P('row', 'col'), may hold values from -6 to 6
- valid_length: int32 [1], replicated, may hold values from 512 to 1024
- norm_gain: float32 [2, 2, 128], replicated, may hold values from 0.1 to 1.9
- norm_bias: float32 [2, 2, 128], replicated, may hold values from -1.5 to 1.5
- proj_weight: bfloat16 [2, 128, 4, 128], replicated, may hold values from -0.5 to 0.5
- gate_weight: bfloat16 [2, 128, 128], replicated, may hold values from -0.5 to 0.5
- out_weight: bfloat16 [2, 128, 128], replicated, may hold values from -0.5 to 0.5
Outputs:
- pair_out: float32 [1024, 1024, 128], P('row', 'col')
The draws below stay inside these ranges and needn't reach their ends.
Inputs may be any that keep to these rules, and one draw needn't show every extreme that they name: Tokens from valid_length on are padding.
All inputs are finite; a program needn't handle non-finite values.
Results may differ from the reference program's by a relative error of at most 0.0039.
Values may be sent and summed in bfloat16 or wider, within the bound.
No kernel may reach another device: no remote copies, remote signals or barrier semaphores. Data moves between devices by JAX's collectives and lax.ppermute only.
A program may use at most 64 MiB of HBM per device.

```python
import jax
import jax.numpy as jnp
from jax import lax

C = 128
TOKENS = 1024


def level_of(key, dims, cuts, least, top_value):
    level = 1.0
    for axis_at, shards_of in cuts:
        heights = jax.random.uniform(jax.random.fold_in(jax.random.fold_in(key, 6), axis_at), (shards_of,), jnp.float32, least / len(cuts), top_value / len(cuts))
        level = level * jnp.repeat(jnp.exp(heights), dims[axis_at] // shards_of).reshape((-1,) + (1,) * (len(dims) - 1 - axis_at))
    return level


def normal_values(rng, dims, scale, reach, split=(), kind=jnp.bfloat16):
    loudness = level_of(rng, dims, split, -0.22, 0.18) if split else 1.0
    array = jax.random.normal(rng, dims, jnp.float32) * scale * loudness
    return jnp.minimum(jnp.maximum(array, -reach), reach).astype(kind)


def setup_inputs(seed: int = 0) -> dict:
    key_of = jax.random.split(jax.random.key(seed), 8)
    pair_map = normal_values(key_of[0], (TOKENS, TOKENS, C), 1.0, 6.0, ((0, 16), (1, 8)), jnp.float32)
    valid_length = jax.random.randint(key_of[1], (1,), TOKENS // 2, TOKENS + 1).astype(jnp.int32)
    norm_gain = jnp.clip(1.0 + 0.18 * jax.random.normal(key_of[2], (2, 2, C), jnp.float32), 0.1, 1.9)
    norm_bias = normal_values(key_of[3], (2, 2, C), 0.3, 1.5, (), jnp.float32)
    proj_weight = normal_values(key_of[4], (2, C, 4, C), C ** -0.5, 0.5)
    gate_weight = normal_values(key_of[5], (2, C, C), C ** -0.5, 0.5)
    out_weight = normal_values(key_of[6], (2, C, C), C ** -0.5, 0.5)
    return dict(pair_map=pair_map, valid_length=valid_length, norm_gain=norm_gain, norm_bias=norm_bias, proj_weight=proj_weight, gate_weight=gate_weight, out_weight=out_weight)


epsilon = 1e-05

def layer_norm(values, gain, offset, axis):
    centre = lax.optimization_barrier(jnp.mean(values, axis=axis, keepdims=True))
    centred = values - centre
    variance = lax.optimization_barrier(jnp.mean(centred * centred, axis=axis, keepdims=True))
    return centred * lax.rsqrt(variance + epsilon) * gain + offset

def reference(pair_map, valid_length, norm_gain, norm_bias, proj_weight, gate_weight, out_weight):
    positions = jnp.arange(TOKENS, dtype=jnp.int32)
    valid = (positions < valid_length[0]).astype(jnp.float32)
    mask = valid[:, None] * valid[None, :]
    state = pair_map
    for layer in range(2):
        normed = layer_norm(state, norm_gain[layer, 0], norm_bias[layer, 0], -1).astype(jnp.bfloat16)
        normed_wide = normed.astype(jnp.float32)
        weights = proj_weight[layer].astype(jnp.float32)
        groups = []
        for group in range(4):
            groups.append(jnp.einsum('ijc,cd->dij', normed_wide, weights[:, group, :]))
        left = (jax.nn.sigmoid(groups[1]) * groups[0] * mask).astype(jnp.bfloat16)
        right = (jax.nn.sigmoid(groups[3]) * groups[2] * mask).astype(jnp.bfloat16)
        groups = None

        def contract(operands):
            if layer == 0:
                total = jnp.dot(operands[0], operands[1].T, preferred_element_type=jnp.float32)
            else:
                total = jnp.dot(operands[0].T, operands[1], preferred_element_type=jnp.float32)
            return total.astype(jnp.bfloat16)
        product = lax.map(contract, (left, right))
        hidden = layer_norm(product.astype(jnp.float32), norm_gain[layer, 1][:, None, None], norm_bias[layer, 1][:, None, None], 0).astype(jnp.bfloat16)
        update_term = jnp.einsum('cij,cd->ijd', hidden.astype(jnp.float32), out_weight[layer].astype(jnp.float32))
        gate_value = jax.nn.sigmoid(jnp.einsum('ijc,cd->ijd', normed_wide, gate_weight[layer].astype(jnp.float32)))
        state = state + gate_value * update_term
    return state
```

```python
import functools

import jax
import jax.numpy as jnp
from jax import lax
from jax.experimental import pallas as pl
from jax.experimental.pallas import tpu as pltpu
from jax.sharding import PartitionSpec as P

epsilon = 1e-05
rows_per_step = 16
mesh_axes = ("row", "col")
vmem_bytes = 48 * 1024 * 1024


def norm_over_channels(values, gain, offset):
    count = values.shape[0]
    centre = jnp.sum(values, axis=0, keepdims=True) * (1.0 / count)
    centred = values - centre
    variance = jnp.sum(centred * centred, axis=0, keepdims=True) * (1.0 / count)
    return centred * lax.rsqrt(variance + epsilon) * gain + offset


def project_pair(normed, row0, weight_ref, mask_args, factor_scratch, n_rows):
    limit, row_base, col_base = mask_args
    channels = weight_ref.shape[1]
    cols = normed.shape[1] // 2
    col_pos = col_base + lax.broadcasted_iota(jnp.int32, (1, cols), 1)
    for side in range(2):
        both = jnp.dot(
            weight_ref[2 * side * channels : 2 * (side + 1) * channels, :],
            normed,
            preferred_element_type=jnp.float32,
        )
        factor = (jnp.tanh(both[channels:]) + 1.0) * both[:channels]
        for t in range(2):
            row = row0 + t
            keep = jnp.logical_and(col_pos < limit, row_base + row < limit).astype(jnp.float32)
            factor_scratch[pl.ds(side * channels * n_rows + row, channels, stride=n_rows), :] = (
                factor[:, t * cols : (t + 1) * cols] * keep
            )


def write_factors(factor_scratch, send_ref):
    channels, sides, n_rows, cols = send_ref.shape
    size = channels * n_rows
    for side in range(sides):
        part = factor_scratch[side * size : (side + 1) * size, :]
        send_ref[:, side] = part.reshape(channels, n_rows, cols).astype(send_ref.dtype)


def mask_positions(place_ref, n_rows):
    return place_ref[0], place_ref[1] + pl.program_id(0) * n_rows, place_ref[2]


def enter_kernel(place_ref, state_ref, weight_ref, affine_ref, send_ref, normed_ref, factor_scratch):
    n_rows = state_ref.shape[0]
    mask_args = mask_positions(place_ref, n_rows)

    def step(pair, carry):
        row0 = pair * 2
        normed = []
        for t in range(2):
            values = state_ref[row0 + t].T
            out = norm_over_channels(values, affine_ref[0], affine_ref[1]).astype(jnp.bfloat16)
            normed_ref[row0 + t] = out
            normed.append(out)
        project_pair(
            jnp.concatenate(normed, axis=1), row0, weight_ref, mask_args, factor_scratch, n_rows
        )
        return carry

    lax.fori_loop(0, n_rows // 2, step, 0)
    write_factors(factor_scratch, send_ref)


def load_returned(returned_ref, product_scratch):
    channels, n_rows, cols = returned_ref.shape
    values = returned_ref[...].astype(jnp.float32)
    product_scratch[...] = values.reshape(channels * n_rows, cols)
    centre = jnp.sum(values, axis=0) * (1.0 / channels)
    centred = product_scratch[...].reshape(channels, n_rows, cols) - centre[None]
    variance = jnp.sum(centred * centred, axis=0) * (1.0 / channels)
    return centre, lax.rsqrt(variance + epsilon)


def update_pair(row0, n_rows, product_scratch, stat_scratch, normed_ref, affine_ref, out_ref, gate_ref):
    channels = out_ref.shape[0]
    hidden = []
    for t in range(2):
        row = row0 + t
        values = product_scratch[pl.ds(row, channels, stride=n_rows), :]
        centre = stat_scratch[0, pl.ds(row, 1), :]
        scale = stat_scratch[1, pl.ds(row, 1), :]
        hidden.append(
            ((values - centre) * scale * affine_ref[2] + affine_ref[3]).astype(jnp.bfloat16)
        )
    term = jnp.dot(
        out_ref[...], jnp.concatenate(hidden, axis=1), preferred_element_type=jnp.float32
    )
    normed = jnp.concatenate([normed_ref[row0], normed_ref[row0 + 1]], axis=1)
    gate = jnp.tanh(jnp.dot(gate_ref[...], normed, preferred_element_type=jnp.float32)) + 1.0
    return gate * term


def middle_kernel(
    place_ref,
    returned_ref,
    state_ref,
    normed_in_ref,
    affine_ref,
    out_weight_ref,
    gate_weight_ref,
    next_weight_ref,
    next_affine_ref,
    send_ref,
    normed_ref,
    new_state_ref,
    factor_scratch,
    product_scratch,
    stat_scratch,
):
    n_rows, channels, cols = new_state_ref.shape
    mask_args = mask_positions(place_ref, n_rows)
    centre, scale = load_returned(returned_ref, product_scratch)
    stat_scratch[0] = centre
    stat_scratch[1] = scale

    def step(pair, carry):
        row0 = pair * 2
        term = update_pair(
            row0,
            n_rows,
            product_scratch,
            stat_scratch,
            normed_in_ref,
            affine_ref,
            out_weight_ref,
            gate_weight_ref,
        )
        normed = []
        for t in range(2):
            values = state_ref[row0 + t].T + term[:, t * cols : (t + 1) * cols]
            new_state_ref[row0 + t] = values
            out = norm_over_channels(values, next_affine_ref[0], next_affine_ref[1])
            out = out.astype(jnp.bfloat16)
            normed_ref[row0 + t] = out
            normed.append(out)
        project_pair(
            jnp.concatenate(normed, axis=1),
            row0,
            next_weight_ref,
            mask_args,
            factor_scratch,
            n_rows,
        )
        return carry

    lax.fori_loop(0, n_rows // 2, step, 0)
    write_factors(factor_scratch, send_ref)


def leave_kernel(
    returned_ref,
    state_ref,
    normed_in_ref,
    affine_ref,
    out_weight_ref,
    gate_weight_ref,
    result_ref,
    product_scratch,
    stat_scratch,
):
    n_rows, cols, channels = result_ref.shape
    centre, scale = load_returned(returned_ref, product_scratch)
    stat_scratch[0] = centre
    stat_scratch[1] = scale

    def step(pair, carry):
        row0 = pair * 2
        term = update_pair(
            row0,
            n_rows,
            product_scratch,
            stat_scratch,
            normed_in_ref,
            affine_ref,
            out_weight_ref,
            gate_weight_ref,
        )
        for t in range(2):
            values = state_ref[row0 + t] + term[:, t * cols : (t + 1) * cols]
            result_ref[row0 + t] = values.T
        return carry

    lax.fori_loop(0, n_rows // 2, step, 0)


def triangle_kernel(n_row, n_col, incoming, left_ref, right_ref, send_ref, left_mat, right_mat):
    tile_rows, tile_cols = left_ref.shape[2:]
    for r in range(n_row):
        for s in range(n_col):
            place = (slice(r * tile_rows, (r + 1) * tile_rows), slice(s * tile_cols, (s + 1) * tile_cols))
            left_mat[place] = left_ref[r * n_col + s, 0]
            right_mat[place] = right_ref[r * n_col + s, 0]
    block = 4 * tile_rows
    for b in range(n_row // 4):
        if incoming:
            product = lax.dot_general(
                left_mat[:, b * block : (b + 1) * block],
                right_mat[...],
                (((0,), (0,)), ((), ())),
                preferred_element_type=jnp.float32,
            )
        else:
            product = lax.dot_general(
                left_mat[b * block : (b + 1) * block, :],
                right_mat[...],
                (((1,), (1,)), ((), ())),
                preferred_element_type=jnp.float32,
            )
        product = product.astype(send_ref.dtype)
        for r in range(4):
            for s in range(n_col):
                send_ref[(b * 4 + r) * n_col + s] = product[
                    r * tile_rows : (r + 1) * tile_rows, s * tile_cols : (s + 1) * tile_cols
                ]


def per_device(pair_map, valid_length, norm_gain, norm_bias, proj_weight, gate_weight, out_weight):
    tile_rows, tile_cols, channels = pair_map.shape
    n_row = lax.axis_size("row")
    n_col = lax.axis_size("col")
    n_dev = n_row * n_col
    n_rows = rows_per_step
    grid = (tile_rows // n_rows,)
    place = jnp.concatenate(
        [
            valid_length,
            jnp.stack([lax.axis_index("row") * tile_rows, lax.axis_index("col") * tile_cols]),
        ]
    ).astype(jnp.int32)
    project = (
        proj_weight.transpose(0, 2, 3, 1).reshape(2, 4 * channels, channels) * jnp.bfloat16(0.5)
    )
    gates = gate_weight.transpose(0, 2, 1) * jnp.bfloat16(0.5)
    outs = out_weight.transpose(0, 2, 1) * jnp.bfloat16(0.5)
    affine = jnp.stack([norm_gain, norm_bias], axis=2).reshape(2, 4, channels, 1)
    affine = jnp.broadcast_to(affine, (2, 4, channels, tile_cols))

    params = pltpu.CompilerParams(
        dimension_semantics=("arbitrary",), vmem_limit_bytes=vmem_bytes
    )
    smem = pl.BlockSpec(memory_space=pltpu.SMEM)

    def whole(array):
        return pl.BlockSpec(array.shape, lambda i: (0,) * array.ndim)

    state_spec = pl.BlockSpec((n_rows, tile_cols, channels), lambda i: (i, 0, 0))
    turned_spec = pl.BlockSpec((n_rows, channels, tile_cols), lambda i: (i, 0, 0))
    send_spec = pl.BlockSpec((channels, 2, n_rows, tile_cols), lambda i: (0, 0, i, 0))
    returned_spec = pl.BlockSpec((channels, n_rows, tile_cols), lambda i: (0, i, 0))
    send_shape = jax.ShapeDtypeStruct((channels, 2, tile_rows, tile_cols), jnp.bfloat16)
    normed_shape = jax.ShapeDtypeStruct((tile_rows, channels, tile_cols), jnp.bfloat16)
    turned_shape = jax.ShapeDtypeStruct((tile_rows, channels, tile_cols), jnp.float32)
    factor_scratch = pltpu.VMEM((2 * channels * n_rows, tile_cols), jnp.float32)
    product_scratch = pltpu.VMEM((channels * n_rows, tile_cols), jnp.float32)
    stat_scratch = pltpu.VMEM((2, n_rows, tile_cols), jnp.float32)

    def exchange(blocks):
        return lax.all_to_all(blocks, mesh_axes, 0, 0, tiled=True)

    def triangle(received, incoming):
        side_spec = lambda side: pl.BlockSpec(
            (n_dev, 1, tile_rows, tile_cols), lambda i: (0, side, 0, 0)
        )
        return pl.pallas_call(
            functools.partial(triangle_kernel, n_row, n_col, incoming),
            grid=(1,),
            out_shape=jax.ShapeDtypeStruct((n_dev, tile_rows, tile_cols), jnp.bfloat16),
            in_specs=[side_spec(0), side_spec(1)],
            out_specs=pl.BlockSpec((n_dev, tile_rows, tile_cols), lambda i: (0, 0, 0)),
            scratch_shapes=[
                pltpu.VMEM((n_row * tile_rows, n_col * tile_cols), jnp.bfloat16),
                pltpu.VMEM((n_row * tile_rows, n_col * tile_cols), jnp.bfloat16),
            ],
            compiler_params=params,
        )(received, received)

    send, normed = pl.pallas_call(
        enter_kernel,
        grid=grid,
        out_shape=[send_shape, normed_shape],
        in_specs=[smem, state_spec, whole(project[0]), whole(affine[0])],
        out_specs=[send_spec, turned_spec],
        scratch_shapes=[factor_scratch],
        compiler_params=params,
    )(place, pair_map, project[0], affine[0])
    returned = exchange(triangle(exchange(send), False))

    send, next_normed, state = pl.pallas_call(
        middle_kernel,
        grid=grid,
        out_shape=[send_shape, normed_shape, turned_shape],
        in_specs=[
            smem,
            returned_spec,
            state_spec,
            turned_spec,
            whole(affine[0]),
            whole(outs[0]),
            whole(gates[0]),
            whole(project[1]),
            whole(affine[1]),
        ],
        out_specs=[send_spec, turned_spec, turned_spec],
        scratch_shapes=[factor_scratch, product_scratch, stat_scratch],
        compiler_params=params,
    )(
        place,
        returned,
        pair_map,
        normed,
        affine[0],
        outs[0],
        gates[0],
        project[1],
        affine[1],
    )
    returned = exchange(triangle(exchange(send), True))

    return pl.pallas_call(
        leave_kernel,
        grid=grid,
        out_shape=jax.ShapeDtypeStruct((tile_rows, tile_cols, channels), jnp.float32),
        in_specs=[
            returned_spec,
            turned_spec,
            turned_spec,
            whole(affine[1]),
            whole(outs[1]),
            whole(gates[1]),
        ],
        out_specs=state_spec,
        scratch_shapes=[product_scratch, stat_scratch],
        compiler_params=params,
    )(returned, state, next_normed, affine[1], outs[1], gates[1])


def solution(mesh):
    placed = (P("row", "col", None), P(), P(), P(), P(), P(), P())
    return jax.shard_map(
        per_device, mesh=mesh, in_specs=placed, out_specs=P("row", "col", None), check_vma=False
    )
```

```python
import functools

import jax
import jax.numpy as jnp
from jax import lax
from jax.experimental import pallas as pl
from jax.experimental.pallas import tpu as pltpu
from jax.sharding import PartitionSpec as P

epsilon = 1e-05
block_rows = 16
spaced = 24
mesh_axes = ("row", "col")
vmem_bytes = 28 * 1024 * 1024
enter_vmem_bytes = 46 * 1024 * 1024


def norm_over_channels(values, gain, offset):
    count = values.shape[0]
    centre = jnp.sum(values, axis=0, keepdims=True) * (1.0 / count)
    centred = values - centre
    variance = jnp.sum(centred * centred, axis=0, keepdims=True) * (1.0 / count)
    return centred * lax.rsqrt(variance + epsilon) * gain + offset


def project_block(row0, place_ref, normed_ref, weight_ref, send_ref, factor_scratch):
    channels, cols = normed_ref.shape[1:]
    limit, row_base, col_base = place_ref[0], place_ref[1] + row0, place_ref[2]
    col_pos = col_base + lax.broadcasted_iota(jnp.int32, (1, cols), 1)

    def pair(p):
        row = 2 * p
        normed = jnp.concatenate([normed_ref[row0 + row], normed_ref[row0 + row + 1]], axis=1)
        for side in range(2):
            both = jnp.dot(
                weight_ref[2 * side * channels : 2 * (side + 1) * channels, :],
                normed,
                preferred_element_type=jnp.float32,
            )
            factor = (jnp.tanh(both[channels:]) + 1.0) * both[:channels]
            for t in range(2):
                keep = jnp.logical_and(col_pos < limit, row_base + row + t < limit)
                factor_scratch[
                    pl.ds(side * channels * spaced + row + t, channels, stride=spaced), :
                ] = factor[:, t * cols : (t + 1) * cols] * keep.astype(jnp.float32)

    for p in range(block_rows // 2):
        pair(p)
    size = channels * spaced
    for side in range(2):
        part = factor_scratch[side * size : (side + 1) * size, :].reshape(channels, spaced, cols)
        send_ref[:, side, pl.ds(row0, block_rows), :] = part[:, :block_rows].astype(send_ref.dtype)


def update_block(
    row0, returned_ref, normed_ref, affine_ref, out_ref, gate_ref, product_scratch, use_row
):
    channels, cols = normed_ref.shape[1:]
    values = returned_ref[:, pl.ds(row0, block_rows), :].astype(jnp.float32)
    for c in range(channels):
        product_scratch[c * spaced : c * spaced + block_rows, :] = values[c]
    centre = jnp.sum(values, axis=0) * (1.0 / channels)
    variance = jnp.zeros_like(centre)
    for c in range(channels):
        centred = product_scratch[c * spaced : c * spaced + block_rows, :] - centre
        variance = variance + centred * centred
    scale = lax.rsqrt(variance * (1.0 / channels) + epsilon)
    for p in range(block_rows // 2):
        row = 2 * p
        hidden = []
        for t in range(2):
            values = product_scratch[pl.ds(row + t, channels, stride=spaced), :]
            centred = values - centre[row + t : row + t + 1]
            out = centred * scale[row + t : row + t + 1] * affine_ref[2] + affine_ref[3]
            hidden.append(out.astype(jnp.bfloat16))
        term = jnp.dot(
            out_ref[...], jnp.concatenate(hidden, axis=1), preferred_element_type=jnp.float32
        )
        normed = jnp.concatenate([normed_ref[row0 + row], normed_ref[row0 + row + 1]], axis=1)
        gate = jnp.tanh(jnp.dot(gate_ref[...], normed, preferred_element_type=jnp.float32)) + 1.0
        term = gate * term
        for t in range(2):
            use_row(row0 + row + t, term[:, t * cols : (t + 1) * cols])


def over_blocks(n_rows, step):
    def body(b, carry):
        step(b, pl.multiple_of(b * block_rows, block_rows))
        return carry

    lax.fori_loop(0, n_rows // block_rows, body, 0)


def enter_kernel(
    place_ref, state_ref, weight_ref, affine_ref, send_ref, normed_ref, state_buf, sems, factor_scratch
):
    n_rows = state_buf.shape[0]

    def fetch(b):
        rows = pl.ds(b * block_rows, block_rows)
        return pltpu.make_async_copy(state_ref.at[rows], state_buf.at[rows], sems.at[b])

    for b in range(n_rows // block_rows):
        fetch(b).start()

    def step(b, row0):
        fetch(b).wait()
        for t in range(block_rows):
            out = norm_over_channels(state_buf[row0 + t].T, affine_ref[0], affine_ref[1])
            normed_ref[row0 + t] = out.astype(jnp.bfloat16)
        project_block(row0, place_ref, normed_ref, weight_ref, send_ref, factor_scratch)

    over_blocks(n_rows, step)


def middle_kernel(
    place_ref,
    returned_ref,
    state_ref,
    normed_in_ref,
    affine_ref,
    out_weight_ref,
    gate_weight_ref,
    next_weight_ref,
    next_affine_ref,
    send_ref,
    normed_ref,
    new_state_ref,
    factor_scratch,
    product_scratch,
):
    def step(b, row0):
        def use_row(row, term):
            new_state_ref[row] = state_ref[row].T + term

        update_block(
            row0,
            returned_ref,
            normed_in_ref,
            affine_ref,
            out_weight_ref,
            gate_weight_ref,
            product_scratch,
            use_row,
        )
        for t in range(block_rows):
            out = norm_over_channels(
                new_state_ref[row0 + t], next_affine_ref[0], next_affine_ref[1]
            )
            normed_ref[row0 + t] = out.astype(jnp.bfloat16)
        project_block(row0, place_ref, normed_ref, next_weight_ref, send_ref, factor_scratch)

    over_blocks(new_state_ref.shape[0], step)


def leave_kernel(
    returned_ref,
    state_ref,
    normed_in_ref,
    affine_ref,
    out_weight_ref,
    gate_weight_ref,
    result_ref,
    result_buf,
    sems,
    product_scratch,
):
    n_rows = result_buf.shape[0]

    def store(b):
        rows = pl.ds(b * block_rows, block_rows)
        return pltpu.make_async_copy(result_buf.at[rows], result_ref.at[rows], sems.at[b])

    def step(b, row0):
        def use_row(row, term):
            result_buf[row] = (state_ref[row] + term).T

        update_block(
            row0,
            returned_ref,
            normed_in_ref,
            affine_ref,
            out_weight_ref,
            gate_weight_ref,
            product_scratch,
            use_row,
        )
        store(b).start()

    over_blocks(n_rows, step)
    for b in range(n_rows // block_rows):
        store(b).wait()


def triangle_kernel(n_row, n_col, incoming, received_ref, send_ref, left_mat, right_mat):
    tile_rows, tile_cols = received_ref.shape[2:]
    for r in range(n_row):
        for s in range(n_col):
            place = (slice(r * tile_rows, (r + 1) * tile_rows), slice(s * tile_cols, (s + 1) * tile_cols))
            left_mat[place] = received_ref[r * n_col + s, 0]
            right_mat[place] = received_ref[r * n_col + s, 1]
    block = 4 * tile_rows
    for b in range(n_row // 4):
        if incoming:
            product = lax.dot_general(
                left_mat[:, b * block : (b + 1) * block],
                right_mat[...],
                (((0,), (0,)), ((), ())),
                preferred_element_type=jnp.float32,
            )
        else:
            product = lax.dot_general(
                left_mat[b * block : (b + 1) * block, :],
                right_mat[...],
                (((1,), (1,)), ((), ())),
                preferred_element_type=jnp.float32,
            )
        product = product.astype(send_ref.dtype)
        for r in range(4):
            for s in range(n_col):
                send_ref[(b * 4 + r) * n_col + s] = product[
                    r * tile_rows : (r + 1) * tile_rows, s * tile_cols : (s + 1) * tile_cols
                ]


def per_device(pair_map, valid_length, norm_gain, norm_bias, proj_weight, gate_weight, out_weight):
    tile_rows, tile_cols, channels = pair_map.shape
    n_row = lax.axis_size("row")
    n_col = lax.axis_size("col")
    n_dev = n_row * n_col
    place = jnp.concatenate(
        [
            valid_length,
            jnp.stack([lax.axis_index("row") * tile_rows, lax.axis_index("col") * tile_cols]),
        ]
    ).astype(jnp.int32)
    project = (
        proj_weight.transpose(0, 2, 3, 1).reshape(2, 4 * channels, channels) * jnp.bfloat16(0.5)
    )
    gates = gate_weight.transpose(0, 2, 1) * jnp.bfloat16(0.5)
    outs = out_weight.transpose(0, 2, 1) * jnp.bfloat16(0.5)
    affine = jnp.stack([norm_gain, norm_bias], axis=2).reshape(2, 4, channels, 1)
    affine = jnp.broadcast_to(affine, (2, 4, channels, tile_cols))

    params = pltpu.CompilerParams(vmem_limit_bytes=vmem_bytes)
    enter_params = pltpu.CompilerParams(vmem_limit_bytes=enter_vmem_bytes)
    smem = pl.BlockSpec(memory_space=pltpu.SMEM)
    vmem = pl.BlockSpec(memory_space=pltpu.VMEM)
    outside = pl.BlockSpec(memory_space=pltpu.HBM)
    send_shape = jax.ShapeDtypeStruct((channels, 2, tile_rows, tile_cols), jnp.bfloat16)
    normed_shape = jax.ShapeDtypeStruct((tile_rows, channels, tile_cols), jnp.bfloat16)
    turned_shape = jax.ShapeDtypeStruct((tile_rows, channels, tile_cols), jnp.float32)
    state_shape = (tile_rows, tile_cols, channels)
    factor_scratch = pltpu.VMEM((2 * channels * spaced, tile_cols), jnp.float32)
    product_scratch = pltpu.VMEM((channels * spaced, tile_cols), jnp.float32)
    copies = pltpu.SemaphoreType.DMA((tile_rows // block_rows,))

    def exchange(blocks):
        return lax.all_to_all(blocks, mesh_axes, 0, 0, tiled=True)

    def triangle(received, incoming):
        whole = pltpu.VMEM((n_row * tile_rows, n_col * tile_cols), jnp.bfloat16)
        return pl.pallas_call(
            functools.partial(triangle_kernel, n_row, n_col, incoming),
            out_shape=jax.ShapeDtypeStruct((n_dev, tile_rows, tile_cols), jnp.bfloat16),
            in_specs=[vmem],
            out_specs=vmem,
            scratch_shapes=[whole, whole],
            compiler_params=params,
        )(received)

    send, normed = pl.pallas_call(
        enter_kernel,
        out_shape=[send_shape, normed_shape],
        in_specs=[smem, outside, vmem, vmem],
        out_specs=[vmem, vmem],
        scratch_shapes=[pltpu.VMEM(state_shape, jnp.float32), copies, factor_scratch],
        compiler_params=enter_params,
    )(place, pair_map, project[0], affine[0])
    returned = exchange(triangle(exchange(send), False))

    send, next_normed, state = pl.pallas_call(
        middle_kernel,
        out_shape=[send_shape, normed_shape, turned_shape],
        in_specs=[smem] + [vmem] * 8,
        out_specs=[vmem, vmem, vmem],
        scratch_shapes=[factor_scratch, product_scratch],
        compiler_params=params,
    )(
        place,
        returned,
        pair_map,
        normed,
        affine[0],
        outs[0],
        gates[0],
        project[1],
        affine[1],
    )
    returned = exchange(triangle(exchange(send), True))

    return pl.pallas_call(
        leave_kernel,
        out_shape=jax.ShapeDtypeStruct(state_shape, jnp.float32),
        in_specs=[vmem] * 6,
        out_specs=outside,
        scratch_shapes=[pltpu.VMEM(state_shape, jnp.float32), copies, product_scratch],
        compiler_params=params,
    )(returned, state, next_normed, affine[1], outs[1], gates[1])


def solution(mesh):
    placed = (P("row", "col", None), P(), P(), P(), P(), P(), P())
    return jax.shard_map(
        per_device, mesh=mesh, in_specs=placed, out_specs=P("row", "col", None), check_vma=False
    )
```

```python
import functools

import jax
import jax.numpy as jnp
from jax import lax
from jax.experimental import pallas as pl
from jax.experimental.pallas import tpu as pltpu
from jax.sharding import PartitionSpec as P

epsilon = 1e-05
block_rows = 16
spaced = 24
mesh_axes = ("row", "col")
vmem_bytes = 20 * 1024 * 1024
enter_vmem_bytes = 46 * 1024 * 1024


def norm_over_channels(values, gain, offset):
    count = values.shape[0]
    centre = jnp.sum(values, axis=0, keepdims=True) * (1.0 / count)
    centred = values - centre
    variance = jnp.sum(centred * centred, axis=0, keepdims=True) * (1.0 / count)
    return centred * lax.rsqrt(variance + epsilon) * gain + offset


def turn_weights(layer, place_in, place_out):
    channels = place_in.shape[1]
    if len(place_in.shape) == 4:
        raw = place_in[layer].astype(jnp.float32) * 0.5
        for g in range(place_in.shape[2]):
            place_out[g * channels : (g + 1) * channels, :] = raw[:, g, :].T.astype(jnp.bfloat16)
    else:
        place_out[...] = (place_in[layer].astype(jnp.float32) * 0.5).T.astype(jnp.bfloat16)


def turn_affine(layer, which, gain_ref, bias_ref, affine_ref):
    channels, cols = affine_ref.shape[1:]
    for at, ref in enumerate((gain_ref, bias_ref)):
        line = ref[layer, which : which + 1, :]
        affine_ref[at] = jnp.broadcast_to(line, (cols, channels)).T


def project_block(row0, place_ref, normed_ref, weight_ref, send_ref, factor_scratch):
    channels, cols = normed_ref.shape[1:]
    limit, row_base, col_base = place_ref[0], place_ref[1] + row0, place_ref[2]
    col_pos = col_base + lax.broadcasted_iota(jnp.int32, (1, cols), 1)

    def pair(p):
        row = 2 * p
        normed = jnp.concatenate([normed_ref[row0 + row], normed_ref[row0 + row + 1]], axis=1)
        for side in range(2):
            both = jnp.dot(
                weight_ref[2 * side * channels : 2 * (side + 1) * channels, :],
                normed,
                preferred_element_type=jnp.float32,
            )
            factor = (jnp.tanh(both[channels:]) + 1.0) * both[:channels]
            for t in range(2):
                keep = jnp.logical_and(col_pos < limit, row_base + row + t < limit)
                factor_scratch[
                    pl.ds(side * channels * spaced + row + t, channels, stride=spaced), :
                ] = factor[:, t * cols : (t + 1) * cols] * keep.astype(jnp.float32)

    for p in range(block_rows // 2):
        pair(p)
    size = channels * spaced
    for side in range(2):
        part = factor_scratch[side * size : (side + 1) * size, :].reshape(channels, spaced, cols)
        send_ref[:, side, pl.ds(row0, block_rows), :] = part[:, :block_rows].astype(send_ref.dtype)


def update_block(
    row0, returned_ref, normed_ref, affine_ref, out_ref, gate_ref, product_scratch, use_row
):
    channels, cols = normed_ref.shape[1:]
    values = returned_ref[:, pl.ds(row0, block_rows), :].astype(jnp.float32)
    for c in range(channels):
        product_scratch[c * spaced : c * spaced + block_rows, :] = values[c]
    centre = jnp.sum(values, axis=0) * (1.0 / channels)
    variance = jnp.zeros_like(centre)
    for c in range(channels):
        centred = product_scratch[c * spaced : c * spaced + block_rows, :] - centre
        variance = variance + centred * centred
    scale = lax.rsqrt(variance * (1.0 / channels) + epsilon)
    for p in range(block_rows // 2):
        row = 2 * p
        hidden = []
        for t in range(2):
            values = product_scratch[pl.ds(row + t, channels, stride=spaced), :]
            centred = values - centre[row + t : row + t + 1]
            out = centred * scale[row + t : row + t + 1] * affine_ref[0] + affine_ref[1]
            hidden.append(out.astype(jnp.bfloat16))
        term = jnp.dot(
            out_ref[...], jnp.concatenate(hidden, axis=1), preferred_element_type=jnp.float32
        )
        normed = jnp.concatenate([normed_ref[row0 + row], normed_ref[row0 + row + 1]], axis=1)
        gate = jnp.tanh(jnp.dot(gate_ref[...], normed, preferred_element_type=jnp.float32)) + 1.0
        term = gate * term
        for t in range(2):
            use_row(row0 + row + t, term[:, t * cols : (t + 1) * cols])


def over_blocks(n_rows, step):
    def body(b, carry):
        step(b, pl.multiple_of(b * block_rows, block_rows))
        return carry

    lax.fori_loop(0, n_rows // block_rows, body, 0)


def enter_kernel(
    place_ref,
    state_ref,
    project_ref,
    gain_ref,
    bias_ref,
    send_ref,
    normed_ref,
    state_buf,
    sems,
    factor_scratch,
    weight_ref,
    affine_ref,
):
    n_rows = state_buf.shape[0]

    def fetch(b):
        rows = pl.ds(b * block_rows, block_rows)
        return pltpu.make_async_copy(state_ref.at[rows], state_buf.at[rows], sems.at[b])

    for b in range(n_rows // block_rows):
        fetch(b).start()
    turn_weights(0, project_ref, weight_ref)
    turn_affine(0, 0, gain_ref, bias_ref, affine_ref)

    def step(b, row0):
        fetch(b).wait()
        for t in range(block_rows):
            out = norm_over_channels(state_buf[row0 + t].T, affine_ref[0], affine_ref[1])
            normed_ref[row0 + t] = out.astype(jnp.bfloat16)
        project_block(row0, place_ref, normed_ref, weight_ref, send_ref, factor_scratch)

    over_blocks(n_rows, step)


def middle_kernel(
    place_ref,
    returned_ref,
    state_ref,
    normed_in_ref,
    gain_ref,
    bias_ref,
    out_ref,
    gate_ref,
    project_ref,
    send_ref,
    normed_ref,
    new_state_ref,
    factor_scratch,
    product_scratch,
    affine_ref,
    next_affine_ref,
    out_weight_ref,
    gate_weight_ref,
    next_weight_ref,
):
    turn_affine(0, 1, gain_ref, bias_ref, affine_ref)
    turn_affine(1, 0, gain_ref, bias_ref, next_affine_ref)
    turn_weights(0, out_ref, out_weight_ref)
    turn_weights(0, gate_ref, gate_weight_ref)
    turn_weights(1, project_ref, next_weight_ref)

    def step(b, row0):
        def use_row(row, term):
            new_state_ref[row] = state_ref[row].T + term

        update_block(
            row0,
            returned_ref,
            normed_in_ref,
            affine_ref,
            out_weight_ref,
            gate_weight_ref,
            product_scratch,
            use_row,
        )
        for t in range(block_rows):
            out = norm_over_channels(
                new_state_ref[row0 + t], next_affine_ref[0], next_affine_ref[1]
            )
            normed_ref[row0 + t] = out.astype(jnp.bfloat16)
        project_block(row0, place_ref, normed_ref, next_weight_ref, send_ref, factor_scratch)

    over_blocks(new_state_ref.shape[0], step)


def leave_kernel(
    returned_ref,
    state_ref,
    normed_in_ref,
    gain_ref,
    bias_ref,
    out_ref,
    gate_ref,
    result_ref,
    result_buf,
    sems,
    product_scratch,
    affine_ref,
    out_weight_ref,
    gate_weight_ref,
):
    n_rows = result_buf.shape[0]
    turn_affine(1, 1, gain_ref, bias_ref, affine_ref)
    turn_weights(1, out_ref, out_weight_ref)
    turn_weights(1, gate_ref, gate_weight_ref)

    def store(b):
        rows = pl.ds(b * block_rows, block_rows)
        return pltpu.make_async_copy(result_buf.at[rows], result_ref.at[rows], sems.at[b])

    def step(b, row0):
        def use_row(row, term):
            result_buf[row] = (state_ref[row] + term).T

        update_block(
            row0,
            returned_ref,
            normed_in_ref,
            affine_ref,
            out_weight_ref,
            gate_weight_ref,
            product_scratch,
            use_row,
        )
        store(b).start()

    over_blocks(n_rows, step)
    for b in range(n_rows // block_rows):
        store(b).wait()


def triangle_kernel(n_row, n_col, incoming, received_ref, send_ref, left_mat, right_mat):
    tile_rows, tile_cols = received_ref.shape[2:]
    for r in range(n_row):
        for s in range(n_col):
            place = (slice(r * tile_rows, (r + 1) * tile_rows), slice(s * tile_cols, (s + 1) * tile_cols))
            left_mat[place] = received_ref[r * n_col + s, 0]
            right_mat[place] = received_ref[r * n_col + s, 1]
    block = 4 * tile_rows
    for b in range(n_row // 4):
        if incoming:
            product = lax.dot_general(
                left_mat[:, b * block : (b + 1) * block],
                right_mat[...],
                (((0,), (0,)), ((), ())),
                preferred_element_type=jnp.float32,
            )
        else:
            product = lax.dot_general(
                left_mat[b * block : (b + 1) * block, :],
                right_mat[...],
                (((1,), (1,)), ((), ())),
                preferred_element_type=jnp.float32,
            )
        product = product.astype(send_ref.dtype)
        for r in range(4):
            for s in range(n_col):
                send_ref[(b * 4 + r) * n_col + s] = product[
                    r * tile_rows : (r + 1) * tile_rows, s * tile_cols : (s + 1) * tile_cols
                ]


def per_device(pair_map, valid_length, norm_gain, norm_bias, proj_weight, gate_weight, out_weight):
    tile_rows, tile_cols, channels = pair_map.shape
    n_row = lax.axis_size("row")
    n_col = lax.axis_size("col")
    n_dev = n_row * n_col
    place = jnp.concatenate(
        [
            valid_length,
            jnp.stack([lax.axis_index("row") * tile_rows, lax.axis_index("col") * tile_cols]),
        ]
    ).astype(jnp.int32)
    params = pltpu.CompilerParams(vmem_limit_bytes=vmem_bytes)
    enter_params = pltpu.CompilerParams(vmem_limit_bytes=enter_vmem_bytes)
    smem = pl.BlockSpec(memory_space=pltpu.SMEM)
    vmem = pl.BlockSpec(memory_space=pltpu.VMEM)
    outside = pl.BlockSpec(memory_space=pltpu.HBM)
    send_shape = jax.ShapeDtypeStruct((channels, 2, tile_rows, tile_cols), jnp.bfloat16)
    normed_shape = jax.ShapeDtypeStruct((tile_rows, channels, tile_cols), jnp.bfloat16)
    turned_shape = jax.ShapeDtypeStruct((tile_rows, channels, tile_cols), jnp.float32)
    state_shape = (tile_rows, tile_cols, channels)
    factor_scratch = pltpu.VMEM((2 * channels * spaced, tile_cols), jnp.float32)
    product_scratch = pltpu.VMEM((channels * spaced, tile_cols), jnp.float32)
    affine_scratch = pltpu.VMEM((2, channels, tile_cols), jnp.float32)
    square_scratch = pltpu.VMEM((channels, channels), jnp.bfloat16)
    project_scratch = pltpu.VMEM((4 * channels, channels), jnp.bfloat16)
    copies = pltpu.SemaphoreType.DMA((tile_rows // block_rows,))

    def exchange(blocks):
        return lax.all_to_all(blocks, mesh_axes, 0, 0, tiled=True)

    def triangle(received, incoming):
        whole = pltpu.VMEM((n_row * tile_rows, n_col * tile_cols), jnp.bfloat16)
        return pl.pallas_call(
            functools.partial(triangle_kernel, n_row, n_col, incoming),
            out_shape=jax.ShapeDtypeStruct((n_dev, tile_rows, tile_cols), jnp.bfloat16),
            in_specs=[vmem],
            out_specs=vmem,
            scratch_shapes=[whole, whole],
            compiler_params=params,
        )(received)

    send, normed = pl.pallas_call(
        enter_kernel,
        out_shape=[send_shape, normed_shape],
        in_specs=[smem, outside, vmem, vmem, vmem],
        out_specs=[vmem, vmem],
        scratch_shapes=[
            pltpu.VMEM(state_shape, jnp.float32),
            copies,
            factor_scratch,
            project_scratch,
            affine_scratch,
        ],
        compiler_params=enter_params,
    )(place, pair_map, proj_weight, norm_gain, norm_bias)
    returned = exchange(triangle(exchange(send), False))

    send, next_normed, state = pl.pallas_call(
        middle_kernel,
        out_shape=[send_shape, normed_shape, turned_shape],
        in_specs=[smem] + [vmem] * 8,
        out_specs=[vmem, vmem, vmem],
        scratch_shapes=[
            factor_scratch,
            product_scratch,
            affine_scratch,
            affine_scratch,
            square_scratch,
            square_scratch,
            project_scratch,
        ],
        compiler_params=params,
    )(
        place,
        returned,
        pair_map,
        normed,
        norm_gain,
        norm_bias,
        out_weight,
        gate_weight,
        proj_weight,
    )
    returned = exchange(triangle(exchange(send), True))

    return pl.pallas_call(
        leave_kernel,
        out_shape=jax.ShapeDtypeStruct(state_shape, jnp.float32),
        in_specs=[vmem] * 7,
        out_specs=outside,
        scratch_shapes=[
            pltpu.VMEM(state_shape, jnp.float32),
            copies,
            product_scratch,
            affine_scratch,
            square_scratch,
            square_scratch,
        ],
        compiler_params=params,
    )(returned, state, next_normed, norm_gain, norm_bias, out_weight, gate_weight)


def solution(mesh):
    placed = (P("row", "col", None), P(), P(), P(), P(), P(), P())
    return jax.shard_map(
        per_device, mesh=mesh, in_specs=placed, out_specs=P("row", "col", None), check_vma=False
    )
```

```python
import functools

import jax
import jax.numpy as jnp
from jax import lax
from jax.experimental import pallas as pl
from jax.experimental.pallas import tpu as pltpu
from jax.sharding import PartitionSpec as P

epsilon = 1e-05
block_rows = 16
pairs_per_block = block_rows // 2
copy_rows = 4
fetch_sizes = (8, 24, 32)
spaced = 24
mesh_axes = ("row", "col")
vmem_bytes = 20 * 1024 * 1024
enter_vmem_bytes = 46 * 1024 * 1024


def norm_over_channels(values, gain, offset):
    count = values.shape[0]
    centre = jnp.sum(values, axis=0, keepdims=True) * (1.0 / count)
    centred = values - centre
    variance = jnp.sum(centred * centred, axis=0, keepdims=True) * (1.0 / count)
    return centred * lax.rsqrt(variance + epsilon) * gain + offset


def turn_weights(layer, place_in, place_out):
    channels = place_in.shape[1]
    if len(place_in.shape) == 4:
        raw = place_in[layer].astype(jnp.float32) * 0.5
        for g in range(place_in.shape[2]):
            place_out[g * channels : (g + 1) * channels, :] = raw[:, g, :].T.astype(jnp.bfloat16)
    else:
        place_out[...] = (place_in[layer].astype(jnp.float32) * 0.5).T.astype(jnp.bfloat16)


def turn_affine(layer, which, gain_ref, bias_ref, affine_ref):
    channels, cols = affine_ref.shape[1:]
    for at, ref in enumerate((gain_ref, bias_ref)):
        line = ref[layer, which : which + 1, :]
        affine_ref[at] = jnp.broadcast_to(line, (cols, channels)).T


def block_pair(row):
    return row // block_rows, row % block_rows


def project_pair(row, place_ref, normed_ref, weight_ref, factor_scratch):
    channels, cols = normed_ref.shape[1:]
    limit, row_base, col_base = place_ref[0], place_ref[1], place_ref[2]
    col_pos = col_base + lax.broadcasted_iota(jnp.int32, (1, cols), 1)
    block, at = block_pair(row)
    normed = jnp.concatenate([normed_ref[row], normed_ref[row + 1]], axis=1)
    for side in range(2):
        both = jnp.dot(
            weight_ref[2 * side * channels : 2 * (side + 1) * channels, :],
            normed,
            preferred_element_type=jnp.float32,
        )
        factor = (jnp.tanh(both[channels:]) + 1.0) * both[:channels]
        for t in range(2):
            keep = jnp.logical_and(col_pos < limit, row_base + row + t < limit)
            first = side * channels * spaced + at + t
            factor_scratch[block % 2, pl.ds(first, channels, stride=spaced), :] = factor[
                :, t * cols : (t + 1) * cols
            ] * keep.astype(jnp.float32)


def write_part(block, part, factor_scratch, send_ref):
    channels, cols = send_ref.shape[0], send_ref.shape[3]
    some = channels // pairs_per_block
    for side in range(2):
        first = (side * channels + part * some) * spaced
        values = factor_scratch[block % 2, first : first + some * spaced, :]
        values = values.reshape(some, spaced, cols)[:, :block_rows].astype(send_ref.dtype)
        rows = slice(block * block_rows, (block + 1) * block_rows)
        send_ref[part * some : (part + 1) * some, side, rows, :] = values


def sum_part(block, part, sums, returned_ref, product_scratch):
    channels = returned_ref.shape[0]
    some = channels // pairs_per_block
    rows = slice(block * block_rows, (block + 1) * block_rows)
    first = returned_ref[0, rows, :].astype(jnp.float32)
    total, squares = sums
    for c in range(part * some, (part + 1) * some):
        values = returned_ref[c, rows, :].astype(jnp.float32)
        product_scratch[block % 2, c * spaced : c * spaced + block_rows, :] = values
        shifted = values - first
        total = total + shifted
        squares = squares + shifted * shifted
    return total, squares


def finish_sums(block, sums, returned_ref, stat_scratch):
    channels = returned_ref.shape[0]
    rows = slice(block * block_rows, (block + 1) * block_rows)
    shift = sums[0] * (1.0 / channels)
    variance = sums[1] * (1.0 / channels) - shift * shift
    stat_scratch[block % 2, 0] = returned_ref[0, rows, :].astype(jnp.float32) + shift
    stat_scratch[block % 2, 1] = lax.rsqrt(jnp.maximum(variance, 0.0) + epsilon)


def update_pair(row, normed_ref, affine_ref, out_ref, gate_ref, product_scratch, stat_scratch):
    channels = normed_ref.shape[1]
    block, at = block_pair(row)
    hidden = []
    for t in range(2):
        values = product_scratch[block % 2, pl.ds(at + t, channels, stride=spaced), :]
        centre = stat_scratch[block % 2, 0, at + t : at + t + 1, :]
        scale = stat_scratch[block % 2, 1, at + t : at + t + 1, :]
        out = (values - centre) * scale * affine_ref[0] + affine_ref[1]
        hidden.append(out.astype(jnp.bfloat16))
    term = jnp.dot(
        out_ref[...], jnp.concatenate(hidden, axis=1), preferred_element_type=jnp.float32
    )
    normed = jnp.concatenate([normed_ref[row], normed_ref[row + 1]], axis=1)
    gate = jnp.tanh(jnp.dot(gate_ref[...], normed, preferred_element_type=jnp.float32)) + 1.0
    return gate * term


def enter_kernel(
    place_ref,
    state_ref,
    early_ref,
    send_ref,
    normed_ref,
    state_buf,
    sems,
    factor_scratch,
    weight_ref,
    affine_ref,
):
    n_rows = state_buf.shape[0]
    n_pairs = n_rows // 2
    n_blocks = n_rows // block_rows
    starts = [sum(fetch_sizes[:b]) for b in range(len(fetch_sizes))]

    def fetch(b):
        rows = pl.ds(starts[b], fetch_sizes[b])
        return pltpu.make_async_copy(state_ref.at[rows], state_buf.at[rows], sems.at[b])

    for b in range(len(starts)):
        fetch(b).start()
    channels = weight_ref.shape[1]
    for g in range(4):
        raw = early_ref[pl.ds(g, channels, stride=4), :] * 0.5
        weight_ref[g * channels : (g + 1) * channels, :] = raw.T.astype(jnp.bfloat16)
    for at in range(2):
        line = early_ref[4 * channels + at : 4 * channels + at + 1, :]
        affine_ref[at] = jnp.broadcast_to(line, (channels, channels)).T

    def normalise(pair):
        if pair < n_pairs:
            for row in (2 * pair, 2 * pair + 1):
                if row in starts:
                    fetch(starts.index(row)).wait()
                out = norm_over_channels(state_buf[row].T, affine_ref[0], affine_ref[1])
                normed_ref[row] = out.astype(jnp.bfloat16)

    normalise(0)
    for block in range(n_blocks + 1):
        for part in range(pairs_per_block):
            pair = block * pairs_per_block + part
            normalise(pair + 1)
            if block < n_blocks:
                project_pair(2 * pair, place_ref, normed_ref, weight_ref, factor_scratch)
            if block > 0:
                write_part(block - 1, part, factor_scratch, send_ref)


def middle_kernel(
    place_ref,
    returned_ref,
    state_ref,
    normed_in_ref,
    gain_ref,
    bias_ref,
    out_ref,
    gate_ref,
    project_ref,
    send_ref,
    normed_ref,
    new_state_ref,
    factor_scratch,
    product_scratch,
    stat_scratch,
    affine_ref,
    next_affine_ref,
    out_weight_ref,
    gate_weight_ref,
    next_weight_ref,
):
    n_rows, channels, cols = new_state_ref.shape
    n_pairs = n_rows // 2
    n_blocks = n_rows // block_rows
    turn_affine(0, 1, gain_ref, bias_ref, affine_ref)
    turn_affine(1, 0, gain_ref, bias_ref, next_affine_ref)
    turn_weights(0, out_ref, out_weight_ref)
    turn_weights(0, gate_ref, gate_weight_ref)
    turn_weights(1, project_ref, next_weight_ref)
    nothing = jnp.zeros((block_rows, cols), jnp.float32)

    def update(pair):
        row = 2 * pair
        term = update_pair(
            row,
            normed_in_ref,
            affine_ref,
            out_weight_ref,
            gate_weight_ref,
            product_scratch,
            stat_scratch,
        )
        for t in range(2):
            values = state_ref[row + t].T + term[:, t * cols : (t + 1) * cols]
            new_state_ref[row + t] = values
            out = norm_over_channels(values, next_affine_ref[0], next_affine_ref[1])
            normed_ref[row + t] = out.astype(jnp.bfloat16)

    for block in range(n_blocks + 3):
        sums = (nothing, nothing)
        for part in range(pairs_per_block):
            if block < n_blocks:
                sums = sum_part(block, part, sums, returned_ref, product_scratch)
            pair = (block - 1) * pairs_per_block + part
            if 0 <= pair < n_pairs:
                update(pair)
            if 0 <= pair - 1 < n_pairs:
                project_pair(
                    2 * (pair - 1), place_ref, normed_ref, next_weight_ref, factor_scratch
                )
            written = (block - 2) * pairs_per_block + part - 1
            if 0 <= written < n_pairs:
                write_part(
                    written // pairs_per_block, written % pairs_per_block, factor_scratch, send_ref
                )
        if block < n_blocks:
            finish_sums(block, sums, returned_ref, stat_scratch)


def leave_kernel(
    returned_ref,
    state_ref,
    normed_in_ref,
    gain_ref,
    bias_ref,
    out_ref,
    gate_ref,
    result_ref,
    result_buf,
    sems,
    product_scratch,
    stat_scratch,
    affine_ref,
    out_weight_ref,
    gate_weight_ref,
):
    n_rows, cols, channels = result_buf.shape
    n_blocks = n_rows // block_rows
    store_rows = n_rows // sems.shape[0]
    turn_affine(1, 1, gain_ref, bias_ref, affine_ref)
    turn_weights(1, out_ref, out_weight_ref)
    turn_weights(1, gate_ref, gate_weight_ref)
    nothing = jnp.zeros((block_rows, cols), jnp.float32)

    def store(b):
        rows = pl.ds(b * store_rows, store_rows)
        return pltpu.make_async_copy(result_buf.at[rows], result_ref.at[rows], sems.at[b])

    for block in range(n_blocks + 1):
        sums = (nothing, nothing)
        for part in range(pairs_per_block):
            if block < n_blocks:
                sums = sum_part(block, part, sums, returned_ref, product_scratch)
            row = 2 * ((block - 1) * pairs_per_block + part)
            if row >= 0:
                term = update_pair(
                    row,
                    normed_in_ref,
                    affine_ref,
                    out_weight_ref,
                    gate_weight_ref,
                    product_scratch,
                    stat_scratch,
                )
                for t in range(2):
                    values = state_ref[row + t] + term[:, t * cols : (t + 1) * cols]
                    result_buf[row + t] = values.T
                if (row + 2) % store_rows == 0:
                    store(row // store_rows).start()
        if block < n_blocks:
            finish_sums(block, sums, returned_ref, stat_scratch)
    for b in range(sems.shape[0]):
        store(b).wait()


def triangle_kernel(n_row, n_col, incoming, received_ref, send_ref, left_mat, right_mat):
    tile_rows, tile_cols = received_ref.shape[2:]
    for r in range(n_row):
        for s in range(n_col):
            place = (slice(r * tile_rows, (r + 1) * tile_rows), slice(s * tile_cols, (s + 1) * tile_cols))
            left_mat[place] = received_ref[r * n_col + s, 0]
            right_mat[place] = received_ref[r * n_col + s, 1]
    block = 4 * tile_rows
    for b in range(n_row // 4):
        if incoming:
            product = lax.dot_general(
                left_mat[:, b * block : (b + 1) * block],
                right_mat[...],
                (((0,), (0,)), ((), ())),
                preferred_element_type=jnp.float32,
            )
        else:
            product = lax.dot_general(
                left_mat[b * block : (b + 1) * block, :],
                right_mat[...],
                (((1,), (1,)), ((), ())),
                preferred_element_type=jnp.float32,
            )
        product = product.astype(send_ref.dtype)
        for r in range(4):
            for s in range(n_col):
                send_ref[(b * 4 + r) * n_col + s] = product[
                    r * tile_rows : (r + 1) * tile_rows, s * tile_cols : (s + 1) * tile_cols
                ]


def per_device(pair_map, valid_length, norm_gain, norm_bias, proj_weight, gate_weight, out_weight):
    tile_rows, tile_cols, channels = pair_map.shape
    n_row = lax.axis_size("row")
    n_col = lax.axis_size("col")
    n_dev = n_row * n_col
    place = jnp.concatenate(
        [
            valid_length,
            jnp.stack([lax.axis_index("row") * tile_rows, lax.axis_index("col") * tile_cols]),
        ]
    ).astype(jnp.int32)
    params = pltpu.CompilerParams(vmem_limit_bytes=vmem_bytes)
    enter_params = pltpu.CompilerParams(vmem_limit_bytes=enter_vmem_bytes)
    smem = pl.BlockSpec(memory_space=pltpu.SMEM)
    vmem = pl.BlockSpec(memory_space=pltpu.VMEM)
    outside = pl.BlockSpec(memory_space=pltpu.HBM)
    send_shape = jax.ShapeDtypeStruct((channels, 2, tile_rows, tile_cols), jnp.bfloat16)
    normed_shape = jax.ShapeDtypeStruct((tile_rows, channels, tile_cols), jnp.bfloat16)
    turned_shape = jax.ShapeDtypeStruct((tile_rows, channels, tile_cols), jnp.float32)
    state_shape = (tile_rows, tile_cols, channels)
    factor_scratch = pltpu.VMEM((2, 2 * channels * spaced, tile_cols), jnp.float32)
    product_scratch = pltpu.VMEM((2, channels * spaced, tile_cols), jnp.float32)
    stat_scratch = pltpu.VMEM((2, 2, block_rows, tile_cols), jnp.float32)
    affine_scratch = pltpu.VMEM((2, channels, tile_cols), jnp.float32)
    square_scratch = pltpu.VMEM((channels, channels), jnp.bfloat16)
    project_scratch = pltpu.VMEM((4 * channels, channels), jnp.bfloat16)
    copies = pltpu.SemaphoreType.DMA((tile_rows // copy_rows,))

    def exchange(blocks):
        return lax.all_to_all(blocks, mesh_axes, 0, 0, tiled=True)

    def triangle(received, incoming):
        whole = pltpu.VMEM((n_row * tile_rows, n_col * tile_cols), jnp.bfloat16)
        return pl.pallas_call(
            functools.partial(triangle_kernel, n_row, n_col, incoming),
            out_shape=jax.ShapeDtypeStruct((n_dev, tile_rows, tile_cols), jnp.bfloat16),
            in_specs=[vmem],
            out_specs=vmem,
            scratch_shapes=[whole, whole],
            compiler_params=params,
        )(received)

    early = jnp.concatenate(
        [
            proj_weight[0].astype(jnp.float32).reshape(4 * channels, channels),
            norm_gain[0, 0:1],
            norm_bias[0, 0:1],
        ]
    )
    send, normed = pl.pallas_call(
        enter_kernel,
        out_shape=[send_shape, normed_shape],
        in_specs=[smem, outside, vmem],
        out_specs=[vmem, vmem],
        scratch_shapes=[
            pltpu.VMEM(state_shape, jnp.float32),
            pltpu.SemaphoreType.DMA((len(fetch_sizes),)),
            factor_scratch,
            project_scratch,
            affine_scratch,
        ],
        compiler_params=enter_params,
    )(place, pair_map, early)
    returned = exchange(triangle(exchange(send), False))

    send, next_normed, state = pl.pallas_call(
        middle_kernel,
        out_shape=[send_shape, normed_shape, turned_shape],
        in_specs=[smem] + [vmem] * 8,
        out_specs=[vmem, vmem, vmem],
        scratch_shapes=[
            factor_scratch,
            product_scratch,
            stat_scratch,
            affine_scratch,
            affine_scratch,
            square_scratch,
            square_scratch,
            project_scratch,
        ],
        compiler_params=params,
    )(
        place,
        returned,
        pair_map,
        normed,
        norm_gain,
        norm_bias,
        out_weight,
        gate_weight,
        proj_weight,
    )
    returned = exchange(triangle(exchange(send), True))

    return pl.pallas_call(
        leave_kernel,
        out_shape=jax.ShapeDtypeStruct(state_shape, jnp.float32),
        in_specs=[vmem] * 7,
        out_specs=outside,
        scratch_shapes=[
            pltpu.VMEM(state_shape, jnp.float32),
            copies,
            product_scratch,
            stat_scratch,
            affine_scratch,
            square_scratch,
            square_scratch,
        ],
        compiler_params=params,
    )(returned, state, next_normed, norm_gain, norm_bias, out_weight, gate_weight)


def solution(mesh):
    placed = (P("row", "col", None), P(), P(), P(), P(), P(), P())
    return jax.shard_map(
        per_device, mesh=mesh, in_specs=placed, out_specs=P("row", "col", None), check_vma=False
    )
```

```python
import functools

import jax
import jax.numpy as jnp
from jax import lax
from jax.experimental import pallas as pl
from jax.experimental.pallas import tpu as pltpu
from jax.sharding import PartitionSpec as P

epsilon = 1e-05
block_rows = 16
pairs_per_block = block_rows // 2
copy_rows = 4
triangle_parts = 4
fetch_sizes = (8, 24, 32)
spaced = 18
mesh_axes = ("row", "col")
vmem_bytes = 20 * 1024 * 1024
enter_vmem_bytes = 46 * 1024 * 1024


def norm_over_channels(values, gain, offset):
    count = values.shape[0]
    centre = jnp.sum(values, axis=0, keepdims=True) * (1.0 / count)
    centred = values - centre
    variance = jnp.sum(centred * centred, axis=0, keepdims=True) * (1.0 / count)
    return centred * lax.rsqrt(variance + epsilon) * gain + offset


def turn_weights(layer, place_in, place_out):
    channels = place_in.shape[1]
    if len(place_in.shape) == 4:
        raw = place_in[layer].astype(jnp.float32) * 0.5
        for g in range(place_in.shape[2]):
            place_out[g * channels : (g + 1) * channels, :] = raw[:, g, :].T.astype(jnp.bfloat16)
    else:
        place_out[...] = (place_in[layer].astype(jnp.float32) * 0.5).T.astype(jnp.bfloat16)


def turn_affine(layer, which, gain_ref, bias_ref, affine_ref):
    channels, cols = affine_ref.shape[1:]
    for at, ref in enumerate((gain_ref, bias_ref)):
        line = ref[layer, which : which + 1, :]
        affine_ref[at] = jnp.broadcast_to(line, (cols, channels)).T


def block_pair(row):
    return row // block_rows, row % block_rows


def project_pair(row, place_ref, normed_ref, weight_ref, factor_scratch):
    channels, cols = normed_ref.shape[1:]
    limit, row_base, col_base = place_ref[0], place_ref[1], place_ref[2]
    col_pos = col_base + lax.broadcasted_iota(jnp.int32, (1, cols), 1)
    block, at = block_pair(row)
    kept = []
    for t in range(2):
        keep = jnp.logical_and(col_pos < limit, row_base + row + t < limit)
        kept.append(normed_ref[row + t] * keep.astype(jnp.float32).astype(jnp.bfloat16))
    for side in range(2):
        for t in range(2):
            both = jnp.dot(
                weight_ref[2 * side * channels : 2 * (side + 1) * channels, :],
                kept[t],
                preferred_element_type=jnp.float32,
            )
            factor = (jnp.tanh(both[channels:]) + 1.0) * both[:channels]
            first = side * channels * spaced + at + t
            factor_scratch[block % 2, pl.ds(first, channels, stride=spaced), :] = factor


def write_part(block, part, factor_scratch, send_ref):
    channels = send_ref.shape[0]
    some = channels // pairs_per_block
    for side in range(2):
        first = (side * channels + part * some) * spaced
        rows = slice(block * block_rows, (block + 1) * block_rows)
        for c in range(some):
            at = first + c * spaced
            values = factor_scratch[block % 2, at : at + block_rows, :]
            send_ref[part * some + c, side, rows, :] = values.astype(send_ref.dtype)


def sum_part(block, part, sums, returned_ref, product_scratch):
    channels = returned_ref.shape[0]
    some = channels // pairs_per_block
    rows = slice(block * block_rows, (block + 1) * block_rows)
    first = returned_ref[0, rows, :].astype(jnp.float32)
    total, squares = sums
    for c in range(part * some, (part + 1) * some):
        values = returned_ref[c, rows, :].astype(jnp.float32)
        product_scratch[block % 2, c * spaced : c * spaced + block_rows, :] = values
        shifted = values - first
        total = total + shifted
        squares = squares + shifted * shifted
    return total, squares


def finish_sums(block, sums, returned_ref, stat_scratch):
    channels = returned_ref.shape[0]
    rows = slice(block * block_rows, (block + 1) * block_rows)
    shift = sums[0] * (1.0 / channels)
    variance = sums[1] * (1.0 / channels) - shift * shift
    stat_scratch[block % 2, 0] = returned_ref[0, rows, :].astype(jnp.float32) + shift
    stat_scratch[block % 2, 1] = lax.rsqrt(jnp.maximum(variance, 0.0) + epsilon)


def update_pair(row, normed_ref, affine_ref, out_ref, gate_ref, product_scratch, stat_scratch):
    channels = normed_ref.shape[1]
    block, at = block_pair(row)
    hidden = []
    for t in range(2):
        values = product_scratch[block % 2, pl.ds(at + t, channels, stride=spaced), :]
        centre = stat_scratch[block % 2, 0, at + t : at + t + 1, :]
        scale = stat_scratch[block % 2, 1, at + t : at + t + 1, :]
        out = (values - centre) * scale * affine_ref[0] + affine_ref[1]
        hidden.append(out.astype(jnp.bfloat16))
    term = jnp.dot(
        out_ref[...], jnp.concatenate(hidden, axis=1), preferred_element_type=jnp.float32
    )
    normed = jnp.concatenate([normed_ref[row], normed_ref[row + 1]], axis=1)
    gate = jnp.tanh(jnp.dot(gate_ref[...], normed, preferred_element_type=jnp.float32)) + 1.0
    return gate * term


def enter_kernel(
    place_ref,
    state_ref,
    early_ref,
    send_ref,
    normed_ref,
    state_buf,
    sems,
    factor_scratch,
    weight_ref,
    affine_ref,
):
    n_rows = state_buf.shape[0]
    n_pairs = n_rows // 2
    n_blocks = n_rows // block_rows
    starts = [sum(fetch_sizes[:b]) for b in range(len(fetch_sizes))]

    def fetch(b):
        rows = pl.ds(starts[b], fetch_sizes[b])
        return pltpu.make_async_copy(state_ref.at[rows], state_buf.at[rows], sems.at[b])

    for b in range(len(starts)):
        fetch(b).start()
    channels = weight_ref.shape[1]
    for g in range(4):
        raw = early_ref[pl.ds(g, channels, stride=4), :] * 0.5
        weight_ref[g * channels : (g + 1) * channels, :] = raw.T.astype(jnp.bfloat16)
    for at in range(2):
        line = early_ref[4 * channels + at : 4 * channels + at + 1, :]
        affine_ref[at] = jnp.broadcast_to(line, (channels, channels)).T

    def normalise(pair):
        if pair < n_pairs:
            for row in (2 * pair, 2 * pair + 1):
                if row in starts:
                    fetch(starts.index(row)).wait()
                out = norm_over_channels(state_buf[row].T, affine_ref[0], affine_ref[1])
                normed_ref[row] = out.astype(jnp.bfloat16)

    normalise(0)
    for block in range(n_blocks + 1):
        for part in range(pairs_per_block):
            pair = block * pairs_per_block + part
            normalise(pair + 1)
            if block < n_blocks:
                project_pair(2 * pair, place_ref, normed_ref, weight_ref, factor_scratch)
            if block > 0:
                write_part(block - 1, part, factor_scratch, send_ref)


def middle_kernel(
    place_ref,
    returned_ref,
    state_ref,
    normed_in_ref,
    gain_ref,
    bias_ref,
    out_ref,
    gate_ref,
    project_ref,
    send_ref,
    normed_ref,
    new_state_ref,
    factor_scratch,
    product_scratch,
    stat_scratch,
    affine_ref,
    next_affine_ref,
    out_weight_ref,
    gate_weight_ref,
    next_weight_ref,
):
    n_rows, channels, cols = new_state_ref.shape
    n_pairs = n_rows // 2
    n_blocks = n_rows // block_rows
    turn_affine(0, 1, gain_ref, bias_ref, affine_ref)
    turn_affine(1, 0, gain_ref, bias_ref, next_affine_ref)
    turn_weights(0, out_ref, out_weight_ref)
    turn_weights(0, gate_ref, gate_weight_ref)
    turn_weights(1, project_ref, next_weight_ref)
    nothing = jnp.zeros((block_rows, cols), jnp.float32)

    def update(pair):
        row = 2 * pair
        term = update_pair(
            row,
            normed_in_ref,
            affine_ref,
            out_weight_ref,
            gate_weight_ref,
            product_scratch,
            stat_scratch,
        )
        for t in range(2):
            values = state_ref[row + t].T + term[:, t * cols : (t + 1) * cols]
            new_state_ref[row + t] = values
            out = norm_over_channels(values, next_affine_ref[0], next_affine_ref[1])
            normed_ref[row + t] = out.astype(jnp.bfloat16)

    for block in range(n_blocks + 3):
        sums = (nothing, nothing)
        for part in range(pairs_per_block):
            if block < n_blocks:
                sums = sum_part(block, part, sums, returned_ref, product_scratch)
            pair = (block - 1) * pairs_per_block + part
            if 0 <= pair < n_pairs:
                update(pair)
            if 0 <= pair - 1 < n_pairs:
                project_pair(
                    2 * (pair - 1), place_ref, normed_ref, next_weight_ref, factor_scratch
                )
            written = (block - 2) * pairs_per_block + part - 1
            if 0 <= written < n_pairs:
                write_part(
                    written // pairs_per_block, written % pairs_per_block, factor_scratch, send_ref
                )
        if block < n_blocks:
            finish_sums(block, sums, returned_ref, stat_scratch)


def leave_kernel(
    returned_ref,
    state_ref,
    normed_in_ref,
    gain_ref,
    bias_ref,
    out_ref,
    gate_ref,
    result_ref,
    result_buf,
    sems,
    product_scratch,
    stat_scratch,
    affine_ref,
    out_weight_ref,
    gate_weight_ref,
):
    n_rows, cols, channels = result_buf.shape
    n_blocks = n_rows // block_rows
    store_rows = n_rows // sems.shape[0]
    turn_affine(1, 1, gain_ref, bias_ref, affine_ref)
    turn_weights(1, out_ref, out_weight_ref)
    turn_weights(1, gate_ref, gate_weight_ref)
    nothing = jnp.zeros((block_rows, cols), jnp.float32)

    def store(b):
        rows = pl.ds(b * store_rows, store_rows)
        return pltpu.make_async_copy(result_buf.at[rows], result_ref.at[rows], sems.at[b])

    for block in range(n_blocks + 1):
        sums = (nothing, nothing)
        for part in range(pairs_per_block):
            if block < n_blocks:
                sums = sum_part(block, part, sums, returned_ref, product_scratch)
            row = 2 * ((block - 1) * pairs_per_block + part)
            if row >= 0:
                term = update_pair(
                    row,
                    normed_in_ref,
                    affine_ref,
                    out_weight_ref,
                    gate_weight_ref,
                    product_scratch,
                    stat_scratch,
                )
                for t in range(2):
                    values = state_ref[row + t] + term[:, t * cols : (t + 1) * cols]
                    result_buf[row + t] = values.T
                if (row + 2) % store_rows == 0:
                    store(row // store_rows).start()
        if block < n_blocks:
            finish_sums(block, sums, returned_ref, stat_scratch)
    for b in range(sems.shape[0]):
        store(b).wait()


def triangle_kernel(n_row, n_col, incoming, received_ref, send_ref, left_mat, right_mat):
    tile_rows, tile_cols = received_ref.shape[2:]
    n_parts = left_mat.shape[0]
    part_rows = n_row * tile_rows // n_parts

    def stage(side, r, s, place_ref, row0, col0):
        place_ref[row0 : row0 + tile_rows, col0 : col0 + tile_cols] = received_ref[
            r * n_col + s, side
        ]

    def stage_left(part):
        place_ref = left_mat.at[part]
        if incoming:
            per_part = n_col // n_parts
            for r in range(n_row):
                for s in range(per_part):
                    stage(0, r, part * per_part + s, place_ref, r * tile_rows, s * tile_cols)
        else:
            per_part = n_row // n_parts
            for r in range(per_part):
                for s in range(n_col):
                    stage(0, part * per_part + r, s, place_ref, r * tile_rows, s * tile_cols)

    stage_left(0)
    for r in range(n_row):
        for s in range(n_col):
            stage(1, r, s, right_mat, r * tile_rows, s * tile_cols)
    summed = (((0,), (0,)), ((), ())) if incoming else (((1,), (1,)), ((), ()))
    for part in range(n_parts):
        if part + 1 < n_parts:
            stage_left(part + 1)
        product = lax.dot_general(
            left_mat[part], right_mat[...], summed, preferred_element_type=jnp.float32
        ).astype(send_ref.dtype)
        for r in range(part_rows // tile_rows):
            for s in range(n_col):
                send_ref[(part * (part_rows // tile_rows) + r) * n_col + s] = product[
                    r * tile_rows : (r + 1) * tile_rows, s * tile_cols : (s + 1) * tile_cols
                ]


def per_device(pair_map, valid_length, norm_gain, norm_bias, proj_weight, gate_weight, out_weight):
    tile_rows, tile_cols, channels = pair_map.shape
    n_row = lax.axis_size("row")
    n_col = lax.axis_size("col")
    n_dev = n_row * n_col
    place = jnp.concatenate(
        [
            valid_length,
            jnp.stack([lax.axis_index("row") * tile_rows, lax.axis_index("col") * tile_cols]),
        ]
    ).astype(jnp.int32)
    params = pltpu.CompilerParams(vmem_limit_bytes=vmem_bytes)
    enter_params = pltpu.CompilerParams(vmem_limit_bytes=enter_vmem_bytes)
    smem = pl.BlockSpec(memory_space=pltpu.SMEM)
    vmem = pl.BlockSpec(memory_space=pltpu.VMEM)
    outside = pl.BlockSpec(memory_space=pltpu.HBM)
    send_shape = jax.ShapeDtypeStruct((channels, 2, tile_rows, tile_cols), jnp.bfloat16)
    normed_shape = jax.ShapeDtypeStruct((tile_rows, channels, tile_cols), jnp.bfloat16)
    turned_shape = jax.ShapeDtypeStruct((tile_rows, channels, tile_cols), jnp.float32)
    state_shape = (tile_rows, tile_cols, channels)
    factor_scratch = pltpu.VMEM((2, 2 * channels * spaced, tile_cols), jnp.float32)
    product_scratch = pltpu.VMEM((2, channels * spaced, tile_cols), jnp.float32)
    stat_scratch = pltpu.VMEM((2, 2, block_rows, tile_cols), jnp.float32)
    affine_scratch = pltpu.VMEM((2, channels, tile_cols), jnp.float32)
    square_scratch = pltpu.VMEM((channels, channels), jnp.bfloat16)
    project_scratch = pltpu.VMEM((4 * channels, channels), jnp.bfloat16)
    copies = pltpu.SemaphoreType.DMA((tile_rows // copy_rows,))

    def exchange(blocks):
        return lax.all_to_all(blocks, mesh_axes, 0, 0, tiled=True)

    def triangle(received, incoming):
        tokens = n_row * tile_rows
        part = tokens // triangle_parts
        left_shape = (tokens, part) if incoming else (part, tokens)
        return pl.pallas_call(
            functools.partial(triangle_kernel, n_row, n_col, incoming),
            out_shape=jax.ShapeDtypeStruct((n_dev, tile_rows, tile_cols), jnp.bfloat16),
            in_specs=[vmem],
            out_specs=vmem,
            scratch_shapes=[
                pltpu.VMEM((triangle_parts,) + left_shape, jnp.bfloat16),
                pltpu.VMEM((tokens, tokens), jnp.bfloat16),
            ],
            compiler_params=params,
        )(received)

    early = jnp.concatenate(
        [
            proj_weight[0].astype(jnp.float32).reshape(4 * channels, channels),
            norm_gain[0, 0:1],
            norm_bias[0, 0:1],
        ]
    )
    send, normed = pl.pallas_call(
        enter_kernel,
        out_shape=[send_shape, normed_shape],
        in_specs=[smem, outside, vmem],
        out_specs=[vmem, vmem],
        scratch_shapes=[
            pltpu.VMEM(state_shape, jnp.float32),
            pltpu.SemaphoreType.DMA((len(fetch_sizes),)),
            factor_scratch,
            project_scratch,
            affine_scratch,
        ],
        compiler_params=enter_params,
    )(place, pair_map, early)
    returned = exchange(triangle(exchange(send), False))

    send, next_normed, state = pl.pallas_call(
        middle_kernel,
        out_shape=[send_shape, normed_shape, turned_shape],
        in_specs=[smem] + [vmem] * 8,
        out_specs=[vmem, vmem, vmem],
        scratch_shapes=[
            factor_scratch,
            product_scratch,
            stat_scratch,
            affine_scratch,
            affine_scratch,
            square_scratch,
            square_scratch,
            project_scratch,
        ],
        compiler_params=params,
    )(
        place,
        returned,
        pair_map,
        normed,
        norm_gain,
        norm_bias,
        out_weight,
        gate_weight,
        proj_weight,
    )
    returned = exchange(triangle(exchange(send), True))

    return pl.pallas_call(
        leave_kernel,
        out_shape=jax.ShapeDtypeStruct(state_shape, jnp.float32),
        in_specs=[vmem] * 7,
        out_specs=outside,
        scratch_shapes=[
            pltpu.VMEM(state_shape, jnp.float32),
            copies,
            product_scratch,
            stat_scratch,
            affine_scratch,
            square_scratch,
            square_scratch,
        ],
        compiler_params=params,
    )(returned, state, next_normed, norm_gain, norm_bias, out_weight, gate_weight)


def solution(mesh):
    placed = (P("row", "col", None), P(), P(), P(), P(), P(), P())
    return jax.shard_map(
        per_device, mesh=mesh, in_specs=placed, out_specs=P("row", "col", None), check_vma=False
    )
```

```python
import functools

import jax
import jax.numpy as jnp
from jax import lax
from jax.experimental import pallas as pl
from jax.experimental.pallas import tpu as pltpu
from jax.sharding import PartitionSpec as P

epsilon = 1e-05
block_rows = 16
pairs_per_block = block_rows // 2
copy_rows = 4
triangle_parts = 4
fetch_parts = 4
spaced = 18
mesh_axes = ("row", "col")
vmem_bytes = 20 * 1024 * 1024
fetch_vmem_bytes = 48 * 1024 * 1024


def standardise(values):
    count = values.shape[0]
    centre = jnp.sum(values, axis=0, keepdims=True) * (1.0 / count)
    centred = values - centre
    variance = jnp.sum(centred * centred, axis=0, keepdims=True) * (1.0 / count)
    return centred * lax.rsqrt(variance + epsilon)


def norm_over_channels(values, gain, offset):
    return standardise(values) * gain + offset


def turn_weights(layer, place_in, place_out):
    channels = place_in.shape[1]
    if len(place_in.shape) == 4:
        raw = place_in[layer].astype(jnp.float32) * 0.5
        for g in range(place_in.shape[2]):
            place_out[g * channels : (g + 1) * channels, :] = raw[:, g, :].T.astype(jnp.bfloat16)
    else:
        place_out[...] = (place_in[layer].astype(jnp.float32) * 0.5).T.astype(jnp.bfloat16)


def turn_affine(layer, which, gain_ref, bias_ref, affine_ref):
    channels, cols = affine_ref.shape[1:]
    for at, ref in enumerate((gain_ref, bias_ref)):
        line = ref[layer, which : which + 1, :]
        affine_ref[at] = jnp.broadcast_to(line, (cols, channels)).T


def block_pair(row):
    return row // block_rows, row % block_rows


def project_pair(row, place_ref, normed_ref, weight_ref, factor_scratch):
    channels, cols = normed_ref.shape[1:]
    limit, row_base, col_base = place_ref[0], place_ref[1], place_ref[2]
    col_pos = col_base + lax.broadcasted_iota(jnp.int32, (1, cols), 1)
    block, at = block_pair(row)
    kept = []
    for t in range(2):
        keep = jnp.logical_and(col_pos < limit, row_base + row + t < limit)
        kept.append(normed_ref[row + t] * keep.astype(jnp.float32).astype(jnp.bfloat16))
    for side in range(2):
        for t in range(2):
            both = jnp.dot(
                weight_ref[2 * side * channels : 2 * (side + 1) * channels, :],
                kept[t],
                preferred_element_type=jnp.float32,
            )
            factor = (jnp.tanh(both[channels:]) + 1.0) * both[:channels]
            first = side * channels * spaced + at + t
            factor_scratch[block % 2, pl.ds(first, channels, stride=spaced), :] = factor


def write_part(block, part, factor_scratch, send_ref):
    channels = send_ref.shape[0]
    some = channels // pairs_per_block
    for side in range(2):
        first = (side * channels + part * some) * spaced
        rows = slice(block * block_rows, (block + 1) * block_rows)
        for c in range(some):
            at = first + c * spaced
            values = factor_scratch[block % 2, at : at + block_rows, :]
            send_ref[part * some + c, side, rows, :] = values.astype(send_ref.dtype)


def sum_part(block, part, sums, returned_ref, product_scratch):
    channels = returned_ref.shape[0]
    some = channels // pairs_per_block
    rows = slice(block * block_rows, (block + 1) * block_rows)
    first = returned_ref[0, rows, :].astype(jnp.float32)
    total, squares = sums
    for c in range(part * some, (part + 1) * some):
        values = returned_ref[c, rows, :].astype(jnp.float32)
        product_scratch[block % 2, c * spaced : c * spaced + block_rows, :] = values
        shifted = values - first
        total = total + shifted
        squares = squares + shifted * shifted
    return total, squares


def finish_sums(block, sums, returned_ref, stat_scratch):
    channels = returned_ref.shape[0]
    rows = slice(block * block_rows, (block + 1) * block_rows)
    shift = sums[0] * (1.0 / channels)
    variance = sums[1] * (1.0 / channels) - shift * shift
    stat_scratch[block % 2, 0] = returned_ref[0, rows, :].astype(jnp.float32) + shift
    stat_scratch[block % 2, 1] = lax.rsqrt(jnp.maximum(variance, 0.0) + epsilon)


def update_pair(row, normed_ref, affine_ref, out_ref, gate_ref, product_scratch, stat_scratch):
    channels = normed_ref.shape[1]
    block, at = block_pair(row)
    hidden = []
    for t in range(2):
        values = product_scratch[block % 2, pl.ds(at + t, channels, stride=spaced), :]
        centre = stat_scratch[block % 2, 0, at + t : at + t + 1, :]
        scale = stat_scratch[block % 2, 1, at + t : at + t + 1, :]
        out = (values - centre) * scale * affine_ref[0] + affine_ref[1]
        hidden.append(out.astype(jnp.bfloat16))
    term = jnp.dot(
        out_ref[...], jnp.concatenate(hidden, axis=1), preferred_element_type=jnp.float32
    )
    normed = jnp.concatenate([normed_ref[row], normed_ref[row + 1]], axis=1)
    gate = jnp.tanh(jnp.dot(gate_ref[...], normed, preferred_element_type=jnp.float32)) + 1.0
    return gate * term


def fetch_kernel(state_ref, standard_ref, state_buf, sems):
    n_rows = state_buf.shape[0]
    fetch_rows = n_rows // sems.shape[0]

    def fetch(b):
        rows = pl.ds(b * fetch_rows, fetch_rows)
        return pltpu.make_async_copy(state_ref.at[rows], state_buf.at[rows], sems.at[b])

    for b in range(sems.shape[0]):
        fetch(b).start()
    for row in range(n_rows):
        if row % fetch_rows == 0:
            fetch(row // fetch_rows).wait()
        standard_ref[row] = standardise(state_buf[row].T)


def enter_kernel(
    place_ref,
    standard_ref,
    project_ref,
    gain_ref,
    bias_ref,
    send_ref,
    normed_ref,
    factor_scratch,
    weight_ref,
    affine_ref,
):
    n_rows = standard_ref.shape[0]
    n_pairs = n_rows // 2
    n_blocks = n_rows // block_rows
    turn_weights(0, project_ref, weight_ref)
    turn_affine(0, 0, gain_ref, bias_ref, affine_ref)

    def normalise(pair):
        if pair < n_pairs:
            for row in (2 * pair, 2 * pair + 1):
                out = standard_ref[row] * affine_ref[0] + affine_ref[1]
                normed_ref[row] = out.astype(jnp.bfloat16)

    normalise(0)
    for block in range(n_blocks + 1):
        for part in range(pairs_per_block):
            pair = block * pairs_per_block + part
            normalise(pair + 1)
            if block < n_blocks:
                project_pair(2 * pair, place_ref, normed_ref, weight_ref, factor_scratch)
            if block > 0:
                write_part(block - 1, part, factor_scratch, send_ref)


def middle_kernel(
    place_ref,
    returned_ref,
    state_ref,
    normed_in_ref,
    gain_ref,
    bias_ref,
    out_ref,
    gate_ref,
    project_ref,
    send_ref,
    normed_ref,
    new_state_ref,
    factor_scratch,
    product_scratch,
    stat_scratch,
    affine_ref,
    next_affine_ref,
    out_weight_ref,
    gate_weight_ref,
    next_weight_ref,
):
    n_rows, channels, cols = new_state_ref.shape
    n_pairs = n_rows // 2
    n_blocks = n_rows // block_rows
    turn_affine(0, 1, gain_ref, bias_ref, affine_ref)
    turn_affine(1, 0, gain_ref, bias_ref, next_affine_ref)
    turn_weights(0, out_ref, out_weight_ref)
    turn_weights(0, gate_ref, gate_weight_ref)
    turn_weights(1, project_ref, next_weight_ref)
    nothing = jnp.zeros((block_rows, cols), jnp.float32)

    def update(pair):
        row = 2 * pair
        term = update_pair(
            row,
            normed_in_ref,
            affine_ref,
            out_weight_ref,
            gate_weight_ref,
            product_scratch,
            stat_scratch,
        )
        for t in range(2):
            values = state_ref[row + t].T + term[:, t * cols : (t + 1) * cols]
            new_state_ref[row + t] = values
            out = norm_over_channels(values, next_affine_ref[0], next_affine_ref[1])
            normed_ref[row + t] = out.astype(jnp.bfloat16)

    for block in range(n_blocks + 3):
        sums = (nothing, nothing)
        for part in range(pairs_per_block):
            if block < n_blocks:
                sums = sum_part(block, part, sums, returned_ref, product_scratch)
            pair = (block - 1) * pairs_per_block + part
            if 0 <= pair < n_pairs:
                update(pair)
            if 0 <= pair - 1 < n_pairs:
                project_pair(
                    2 * (pair - 1), place_ref, normed_ref, next_weight_ref, factor_scratch
                )
            written = (block - 2) * pairs_per_block + part - 1
            if 0 <= written < n_pairs:
                write_part(
                    written // pairs_per_block, written % pairs_per_block, factor_scratch, send_ref
                )
        if block < n_blocks:
            finish_sums(block, sums, returned_ref, stat_scratch)


def leave_kernel(
    returned_ref,
    state_ref,
    normed_in_ref,
    gain_ref,
    bias_ref,
    out_ref,
    gate_ref,
    result_ref,
    result_buf,
    sems,
    product_scratch,
    stat_scratch,
    affine_ref,
    out_weight_ref,
    gate_weight_ref,
):
    n_rows, cols, channels = result_buf.shape
    n_blocks = n_rows // block_rows
    store_rows = n_rows // sems.shape[0]
    turn_affine(1, 1, gain_ref, bias_ref, affine_ref)
    turn_weights(1, out_ref, out_weight_ref)
    turn_weights(1, gate_ref, gate_weight_ref)
    nothing = jnp.zeros((block_rows, cols), jnp.float32)

    def store(b):
        rows = pl.ds(b * store_rows, store_rows)
        return pltpu.make_async_copy(result_buf.at[rows], result_ref.at[rows], sems.at[b])

    for block in range(n_blocks + 1):
        sums = (nothing, nothing)
        for part in range(pairs_per_block):
            if block < n_blocks:
                sums = sum_part(block, part, sums, returned_ref, product_scratch)
            row = 2 * ((block - 1) * pairs_per_block + part)
            if row >= 0:
                term = update_pair(
                    row,
                    normed_in_ref,
                    affine_ref,
                    out_weight_ref,
                    gate_weight_ref,
                    product_scratch,
                    stat_scratch,
                )
                for t in range(2):
                    values = state_ref[row + t] + term[:, t * cols : (t + 1) * cols]
                    result_buf[row + t] = values.T
                if (row + 2) % store_rows == 0:
                    store(row // store_rows).start()
        if block < n_blocks:
            finish_sums(block, sums, returned_ref, stat_scratch)
    for b in range(sems.shape[0]):
        store(b).wait()


def triangle_kernel(n_row, n_col, incoming, received_ref, send_ref, left_mat, right_mat):
    tile_rows, tile_cols = received_ref.shape[2:]
    n_parts = left_mat.shape[0]
    part_rows = n_row * tile_rows // n_parts

    def stage(side, r, s, place_ref, row0, col0):
        place_ref[row0 : row0 + tile_rows, col0 : col0 + tile_cols] = received_ref[
            r * n_col + s, side
        ]

    def stage_left(part):
        place_ref = left_mat.at[part]
        if incoming:
            per_part = n_col // n_parts
            for r in range(n_row):
                for s in range(per_part):
                    stage(0, r, part * per_part + s, place_ref, r * tile_rows, s * tile_cols)
        else:
            per_part = n_row // n_parts
            for r in range(per_part):
                for s in range(n_col):
                    stage(0, part * per_part + r, s, place_ref, r * tile_rows, s * tile_cols)

    stage_left(0)
    for r in range(n_row):
        for s in range(n_col):
            stage(1, r, s, right_mat, r * tile_rows, s * tile_cols)
    summed = (((0,), (0,)), ((), ())) if incoming else (((1,), (1,)), ((), ()))
    for part in range(n_parts):
        if part + 1 < n_parts:
            stage_left(part + 1)
        product = lax.dot_general(
            left_mat[part], right_mat[...], summed, preferred_element_type=jnp.float32
        ).astype(send_ref.dtype)
        for r in range(part_rows // tile_rows):
            for s in range(n_col):
                send_ref[(part * (part_rows // tile_rows) + r) * n_col + s] = product[
                    r * tile_rows : (r + 1) * tile_rows, s * tile_cols : (s + 1) * tile_cols
                ]


def per_device(pair_map, valid_length, norm_gain, norm_bias, proj_weight, gate_weight, out_weight):
    tile_rows, tile_cols, channels = pair_map.shape
    n_row = lax.axis_size("row")
    n_col = lax.axis_size("col")
    n_dev = n_row * n_col
    place = jnp.concatenate(
        [
            valid_length,
            jnp.stack([lax.axis_index("row") * tile_rows, lax.axis_index("col") * tile_cols]),
        ]
    ).astype(jnp.int32)
    params = pltpu.CompilerParams(vmem_limit_bytes=vmem_bytes)
    smem = pl.BlockSpec(memory_space=pltpu.SMEM)
    vmem = pl.BlockSpec(memory_space=pltpu.VMEM)
    outside = pl.BlockSpec(memory_space=pltpu.HBM)
    send_shape = jax.ShapeDtypeStruct((channels, 2, tile_rows, tile_cols), jnp.bfloat16)
    normed_shape = jax.ShapeDtypeStruct((tile_rows, channels, tile_cols), jnp.bfloat16)
    turned_shape = jax.ShapeDtypeStruct((tile_rows, channels, tile_cols), jnp.float32)
    state_shape = (tile_rows, tile_cols, channels)
    factor_scratch = pltpu.VMEM((2, 2 * channels * spaced, tile_cols), jnp.float32)
    product_scratch = pltpu.VMEM((2, channels * spaced, tile_cols), jnp.float32)
    stat_scratch = pltpu.VMEM((2, 2, block_rows, tile_cols), jnp.float32)
    affine_scratch = pltpu.VMEM((2, channels, tile_cols), jnp.float32)
    square_scratch = pltpu.VMEM((channels, channels), jnp.bfloat16)
    project_scratch = pltpu.VMEM((4 * channels, channels), jnp.bfloat16)
    copies = pltpu.SemaphoreType.DMA((tile_rows // copy_rows,))

    def exchange(blocks):
        return lax.all_to_all(blocks, mesh_axes, 0, 0, tiled=True)

    def triangle(received, incoming):
        tokens = n_row * tile_rows
        part = tokens // triangle_parts
        left_shape = (tokens, part) if incoming else (part, tokens)
        return pl.pallas_call(
            functools.partial(triangle_kernel, n_row, n_col, incoming),
            out_shape=jax.ShapeDtypeStruct((n_dev, tile_rows, tile_cols), jnp.bfloat16),
            in_specs=[vmem],
            out_specs=vmem,
            scratch_shapes=[
                pltpu.VMEM((triangle_parts,) + left_shape, jnp.bfloat16),
                pltpu.VMEM((tokens, tokens), jnp.bfloat16),
            ],
            compiler_params=params,
        )(received)

    standard = pl.pallas_call(
        fetch_kernel,
        out_shape=turned_shape,
        in_specs=[outside],
        out_specs=vmem,
        scratch_shapes=[
            pltpu.VMEM(state_shape, jnp.float32),
            pltpu.SemaphoreType.DMA((fetch_parts,)),
        ],
        compiler_params=pltpu.CompilerParams(vmem_limit_bytes=fetch_vmem_bytes),
    )(pair_map)
    send, normed = pl.pallas_call(
        enter_kernel,
        out_shape=[send_shape, normed_shape],
        in_specs=[smem, vmem, vmem, vmem, vmem],
        out_specs=[vmem, vmem],
        scratch_shapes=[factor_scratch, project_scratch, affine_scratch],
        compiler_params=params,
    )(place, standard, proj_weight, norm_gain, norm_bias)
    returned = exchange(triangle(exchange(send), False))

    send, next_normed, state = pl.pallas_call(
        middle_kernel,
        out_shape=[send_shape, normed_shape, turned_shape],
        in_specs=[smem] + [vmem] * 8,
        out_specs=[vmem, vmem, vmem],
        scratch_shapes=[
            factor_scratch,
            product_scratch,
            stat_scratch,
            affine_scratch,
            affine_scratch,
            square_scratch,
            square_scratch,
            project_scratch,
        ],
        compiler_params=params,
    )(
        place,
        returned,
        pair_map,
        normed,
        norm_gain,
        norm_bias,
        out_weight,
        gate_weight,
        proj_weight,
    )
    returned = exchange(triangle(exchange(send), True))

    return pl.pallas_call(
        leave_kernel,
        out_shape=jax.ShapeDtypeStruct(state_shape, jnp.float32),
        in_specs=[vmem] * 7,
        out_specs=outside,
        scratch_shapes=[
            pltpu.VMEM(state_shape, jnp.float32),
            copies,
            product_scratch,
            stat_scratch,
            affine_scratch,
            square_scratch,
            square_scratch,
        ],
        compiler_params=params,
    )(returned, state, next_normed, norm_gain, norm_bias, out_weight, gate_weight)


def solution(mesh):
    placed = (P("row", "col", None), P(), P(), P(), P(), P(), P())
    return jax.shard_map(
        per_device, mesh=mesh, in_specs=placed, out_specs=P("row", "col", None), check_vma=False
    )
```

```python
import functools

import jax
import jax.numpy as jnp
from jax import lax
from jax.experimental import pallas as pl
from jax.experimental.pallas import tpu as pltpu
from jax.sharding import PartitionSpec as P

epsilon = 1e-05
block_rows = 16
pairs_per_block = block_rows // 2
copy_rows = 4
triangle_parts = 4
fetch_parts = 4
spaced = 18
mesh_axes = ("row", "col")
vmem_bytes = 20 * 1024 * 1024
fetch_vmem_bytes = 48 * 1024 * 1024


def standardise(values):
    count = values.shape[0]
    centre = jnp.sum(values, axis=0, keepdims=True) * (1.0 / count)
    centred = values - centre
    variance = jnp.sum(centred * centred, axis=0, keepdims=True) * (1.0 / count)
    return centred * lax.rsqrt(variance + epsilon)


def norm_over_channels(values, gain, offset):
    return standardise(values) * gain + offset


def turn_weights(layer, place_in, place_out):
    channels = place_in.shape[1]
    if len(place_in.shape) == 4:
        raw = place_in[layer].astype(jnp.float32) * 0.5
        for g in range(place_in.shape[2]):
            place_out[g * channels : (g + 1) * channels, :] = raw[:, g, :].T.astype(jnp.bfloat16)
    else:
        place_out[...] = (place_in[layer].astype(jnp.float32) * 0.5).T.astype(jnp.bfloat16)


def turn_affine(layer, which, gain_ref, bias_ref, affine_ref):
    channels, cols = affine_ref.shape[1:]
    for at, ref in enumerate((gain_ref, bias_ref)):
        line = ref[layer, which : which + 1, :]
        affine_ref[at] = jnp.broadcast_to(line, (cols, channels)).T


def block_pair(row):
    return row // block_rows, row % block_rows


def project_pair(row, place_ref, normed_ref, weight_ref, factor_scratch):
    channels, cols = normed_ref.shape[1:]
    limit, row_base, col_base = place_ref[0], place_ref[1], place_ref[2]
    col_pos = col_base + lax.broadcasted_iota(jnp.int32, (1, cols), 1)
    block, at = block_pair(row)
    kept = []
    for t in range(2):
        keep = jnp.logical_and(col_pos < limit, row_base + row + t < limit)
        kept.append(normed_ref[row + t] * keep.astype(jnp.float32).astype(jnp.bfloat16))
    for side in range(2):
        for t in range(2):
            both = jnp.dot(
                weight_ref[2 * side * channels : 2 * (side + 1) * channels, :],
                kept[t],
                preferred_element_type=jnp.float32,
            )
            factor = (jnp.tanh(both[channels:]) + 1.0) * both[:channels]
            first = side * channels * spaced + at + t
            factor_scratch[block % 2, pl.ds(first, channels, stride=spaced), :] = factor


def write_part(block, part, factor_scratch, send_ref):
    channels = send_ref.shape[0]
    some = channels // pairs_per_block
    for side in range(2):
        first = (side * channels + part * some) * spaced
        rows = slice(block * block_rows, (block + 1) * block_rows)
        for c in range(some):
            at = first + c * spaced
            values = factor_scratch[block % 2, at : at + block_rows, :]
            send_ref[part * some + c, side, rows, :] = values.astype(send_ref.dtype)


def sum_part(block, part, sums, returned_ref, product_scratch):
    channels = returned_ref.shape[0]
    some = channels // pairs_per_block
    rows = slice(block * block_rows, (block + 1) * block_rows)
    first = returned_ref[0, rows, :].astype(jnp.float32)
    total, squares = sums
    for c in range(part * some, (part + 1) * some):
        values = returned_ref[c, rows, :].astype(jnp.float32)
        product_scratch[block % 2, c * spaced : c * spaced + block_rows, :] = values
        shifted = values - first
        total = total + shifted
        squares = squares + shifted * shifted
    return total, squares


def finish_sums(block, sums, returned_ref, stat_scratch):
    channels = returned_ref.shape[0]
    rows = slice(block * block_rows, (block + 1) * block_rows)
    shift = sums[0] * (1.0 / channels)
    variance = sums[1] * (1.0 / channels) - shift * shift
    stat_scratch[block % 2, 0] = returned_ref[0, rows, :].astype(jnp.float32) + shift
    stat_scratch[block % 2, 1] = lax.rsqrt(jnp.maximum(variance, 0.0) + epsilon)


def update_pair(row, normed_ref, affine_ref, out_ref, gate_ref, product_scratch, stat_scratch):
    channels = normed_ref.shape[1]
    block, at = block_pair(row)
    hidden = []
    for t in range(2):
        values = product_scratch[block % 2, pl.ds(at + t, channels, stride=spaced), :]
        centre = stat_scratch[block % 2, 0, at + t : at + t + 1, :]
        scale = stat_scratch[block % 2, 1, at + t : at + t + 1, :]
        out = (values - centre) * scale * affine_ref[0] + affine_ref[1]
        hidden.append(out.astype(jnp.bfloat16))
    term = jnp.dot(
        out_ref[...], jnp.concatenate(hidden, axis=1), preferred_element_type=jnp.float32
    )
    normed = jnp.concatenate([normed_ref[row], normed_ref[row + 1]], axis=1)
    gate = jnp.tanh(jnp.dot(gate_ref[...], normed, preferred_element_type=jnp.float32)) + 1.0
    return gate * term


def fetch_kernel(place_ref, state_ref, standard_ref, state_buf, sems):
    n_rows = state_buf.shape[0]
    fetch_rows = n_rows // sems.shape[0]

    def fetch(b):
        rows = pl.ds(b * fetch_rows, fetch_rows)
        return pltpu.make_async_copy(state_ref.at[rows], state_buf.at[rows], sems.at[b])

    for b in range(sems.shape[0]):
        fetch(b).start()
    for row in range(n_rows):
        if row % fetch_rows == 0:
            fetch(row // fetch_rows).wait()
        standard_ref[row] = standardise(state_buf[row].T)


def enter_kernel(
    place_ref,
    standard_ref,
    project_ref,
    gain_ref,
    bias_ref,
    send_ref,
    normed_ref,
    factor_scratch,
    weight_ref,
    affine_ref,
):
    n_rows = standard_ref.shape[0]
    n_pairs = n_rows // 2
    n_blocks = n_rows // block_rows
    turn_weights(0, project_ref, weight_ref)
    turn_affine(0, 0, gain_ref, bias_ref, affine_ref)

    def normalise(pair):
        if pair < n_pairs:
            for row in (2 * pair, 2 * pair + 1):
                out = standard_ref[row] * affine_ref[0] + affine_ref[1]
                normed_ref[row] = out.astype(jnp.bfloat16)

    normalise(0)
    for block in range(n_blocks + 1):
        for part in range(pairs_per_block):
            pair = block * pairs_per_block + part
            normalise(pair + 1)
            if block < n_blocks:
                project_pair(2 * pair, place_ref, normed_ref, weight_ref, factor_scratch)
            if block > 0:
                write_part(block - 1, part, factor_scratch, send_ref)


def middle_kernel(
    place_ref,
    returned_ref,
    state_ref,
    normed_in_ref,
    gain_ref,
    bias_ref,
    out_ref,
    gate_ref,
    project_ref,
    send_ref,
    normed_ref,
    new_state_ref,
    factor_scratch,
    product_scratch,
    stat_scratch,
    affine_ref,
    next_affine_ref,
    out_weight_ref,
    gate_weight_ref,
    next_weight_ref,
):
    n_rows, channels, cols = new_state_ref.shape
    n_pairs = n_rows // 2
    n_blocks = n_rows // block_rows
    turn_affine(0, 1, gain_ref, bias_ref, affine_ref)
    turn_affine(1, 0, gain_ref, bias_ref, next_affine_ref)
    turn_weights(0, out_ref, out_weight_ref)
    turn_weights(0, gate_ref, gate_weight_ref)
    turn_weights(1, project_ref, next_weight_ref)
    nothing = jnp.zeros((block_rows, cols), jnp.float32)

    def update(pair):
        row = 2 * pair
        term = update_pair(
            row,
            normed_in_ref,
            affine_ref,
            out_weight_ref,
            gate_weight_ref,
            product_scratch,
            stat_scratch,
        )
        for t in range(2):
            values = state_ref[row + t].T + term[:, t * cols : (t + 1) * cols]
            new_state_ref[row + t] = values
            out = norm_over_channels(values, next_affine_ref[0], next_affine_ref[1])
            normed_ref[row + t] = out.astype(jnp.bfloat16)

    for block in range(n_blocks + 3):
        sums = (nothing, nothing)
        for part in range(pairs_per_block):
            if block < n_blocks:
                sums = sum_part(block, part, sums, returned_ref, product_scratch)
            pair = (block - 1) * pairs_per_block + part
            if 0 <= pair < n_pairs:
                update(pair)
            if 0 <= pair - 1 < n_pairs:
                project_pair(
                    2 * (pair - 1), place_ref, normed_ref, next_weight_ref, factor_scratch
                )
            written = (block - 2) * pairs_per_block + part - 1
            if 0 <= written < n_pairs:
                write_part(
                    written // pairs_per_block, written % pairs_per_block, factor_scratch, send_ref
                )
        if block < n_blocks:
            finish_sums(block, sums, returned_ref, stat_scratch)


def leave_kernel(
    returned_ref,
    state_ref,
    normed_in_ref,
    gain_ref,
    bias_ref,
    out_ref,
    gate_ref,
    result_ref,
    result_buf,
    sems,
    product_scratch,
    stat_scratch,
    affine_ref,
    out_weight_ref,
    gate_weight_ref,
):
    n_rows, cols, channels = result_buf.shape
    n_blocks = n_rows // block_rows
    store_rows = n_rows // sems.shape[0]
    turn_affine(1, 1, gain_ref, bias_ref, affine_ref)
    turn_weights(1, out_ref, out_weight_ref)
    turn_weights(1, gate_ref, gate_weight_ref)
    nothing = jnp.zeros((block_rows, cols), jnp.float32)

    def store(b):
        rows = pl.ds(b * store_rows, store_rows)
        return pltpu.make_async_copy(result_buf.at[rows], result_ref.at[rows], sems.at[b])

    for block in range(n_blocks + 1):
        sums = (nothing, nothing)
        for part in range(pairs_per_block):
            if block < n_blocks:
                sums = sum_part(block, part, sums, returned_ref, product_scratch)
            row = 2 * ((block - 1) * pairs_per_block + part)
            if row >= 0:
                term = update_pair(
                    row,
                    normed_in_ref,
                    affine_ref,
                    out_weight_ref,
                    gate_weight_ref,
                    product_scratch,
                    stat_scratch,
                )
                for t in range(2):
                    values = state_ref[row + t] + term[:, t * cols : (t + 1) * cols]
                    result_buf[row + t] = values.T
                if (row + 2) % store_rows == 0:
                    store(row // store_rows).start()
        if block < n_blocks:
            finish_sums(block, sums, returned_ref, stat_scratch)
    for b in range(sems.shape[0]):
        store(b).wait()


def triangle_kernel(n_row, n_col, incoming, received_ref, send_ref, left_mat, right_mat):
    tile_rows, tile_cols = received_ref.shape[2:]
    n_parts = left_mat.shape[0]
    part_rows = n_row * tile_rows // n_parts

    def stage(side, r, s, place_ref, row0, col0):
        place_ref[row0 : row0 + tile_rows, col0 : col0 + tile_cols] = received_ref[
            r * n_col + s, side
        ]

    def stage_left(part):
        place_ref = left_mat.at[part]
        if incoming:
            per_part = n_col // n_parts
            for r in range(n_row):
                for s in range(per_part):
                    stage(0, r, part * per_part + s, place_ref, r * tile_rows, s * tile_cols)
        else:
            per_part = n_row // n_parts
            for r in range(per_part):
                for s in range(n_col):
                    stage(0, part * per_part + r, s, place_ref, r * tile_rows, s * tile_cols)

    stage_left(0)
    for r in range(n_row):
        for s in range(n_col):
            stage(1, r, s, right_mat, r * tile_rows, s * tile_cols)
    summed = (((0,), (0,)), ((), ())) if incoming else (((1,), (1,)), ((), ()))
    for part in range(n_parts):
        if part + 1 < n_parts:
            stage_left(part + 1)
        product = lax.dot_general(
            left_mat[part], right_mat[...], summed, preferred_element_type=jnp.float32
        ).astype(send_ref.dtype)
        for r in range(part_rows // tile_rows):
            for s in range(n_col):
                send_ref[(part * (part_rows // tile_rows) + r) * n_col + s] = product[
                    r * tile_rows : (r + 1) * tile_rows, s * tile_cols : (s + 1) * tile_cols
                ]


def per_device(pair_map, valid_length, norm_gain, norm_bias, proj_weight, gate_weight, out_weight):
    tile_rows, tile_cols, channels = pair_map.shape
    n_row = lax.axis_size("row")
    n_col = lax.axis_size("col")
    n_dev = n_row * n_col
    place = jnp.concatenate(
        [
            valid_length,
            jnp.stack([lax.axis_index("row") * tile_rows, lax.axis_index("col") * tile_cols]),
        ]
    ).astype(jnp.int32)
    params = pltpu.CompilerParams(vmem_limit_bytes=vmem_bytes)
    smem = pl.BlockSpec(memory_space=pltpu.SMEM)
    vmem = pl.BlockSpec(memory_space=pltpu.VMEM)
    outside = pl.BlockSpec(memory_space=pltpu.HBM)
    send_shape = jax.ShapeDtypeStruct((channels, 2, tile_rows, tile_cols), jnp.bfloat16)
    normed_shape = jax.ShapeDtypeStruct((tile_rows, channels, tile_cols), jnp.bfloat16)
    turned_shape = jax.ShapeDtypeStruct((tile_rows, channels, tile_cols), jnp.float32)
    state_shape = (tile_rows, tile_cols, channels)
    factor_scratch = pltpu.VMEM((2, 2 * channels * spaced, tile_cols), jnp.float32)
    product_scratch = pltpu.VMEM((2, channels * spaced, tile_cols), jnp.float32)
    stat_scratch = pltpu.VMEM((2, 2, block_rows, tile_cols), jnp.float32)
    affine_scratch = pltpu.VMEM((2, channels, tile_cols), jnp.float32)
    square_scratch = pltpu.VMEM((channels, channels), jnp.bfloat16)
    project_scratch = pltpu.VMEM((4 * channels, channels), jnp.bfloat16)
    copies = pltpu.SemaphoreType.DMA((tile_rows // copy_rows,))

    def exchange(blocks):
        return lax.all_to_all(blocks, mesh_axes, 0, 0, tiled=True)

    def triangle(received, incoming):
        tokens = n_row * tile_rows
        part = tokens // triangle_parts
        left_shape = (tokens, part) if incoming else (part, tokens)
        return pl.pallas_call(
            functools.partial(triangle_kernel, n_row, n_col, incoming),
            out_shape=jax.ShapeDtypeStruct((n_dev, tile_rows, tile_cols), jnp.bfloat16),
            in_specs=[vmem],
            out_specs=vmem,
            scratch_shapes=[
                pltpu.VMEM((triangle_parts,) + left_shape, jnp.bfloat16),
                pltpu.VMEM((tokens, tokens), jnp.bfloat16),
            ],
            compiler_params=params,
        )(received)

    standard = pl.pallas_call(
        fetch_kernel,
        out_shape=turned_shape,
        in_specs=[smem, outside],
        out_specs=vmem,
        scratch_shapes=[
            pltpu.VMEM(state_shape, jnp.float32),
            pltpu.SemaphoreType.DMA((fetch_parts,)),
        ],
        compiler_params=pltpu.CompilerParams(vmem_limit_bytes=fetch_vmem_bytes),
    )(place, pair_map)
    send, normed = pl.pallas_call(
        enter_kernel,
        out_shape=[send_shape, normed_shape],
        in_specs=[smem, vmem, vmem, vmem, vmem],
        out_specs=[vmem, vmem],
        scratch_shapes=[factor_scratch, project_scratch, affine_scratch],
        compiler_params=params,
    )(place, standard, proj_weight, norm_gain, norm_bias)
    returned = exchange(triangle(exchange(send), False))

    send, next_normed, state = pl.pallas_call(
        middle_kernel,
        out_shape=[send_shape, normed_shape, turned_shape],
        in_specs=[smem] + [vmem] * 8,
        out_specs=[vmem, vmem, vmem],
        scratch_shapes=[
            factor_scratch,
            product_scratch,
            stat_scratch,
            affine_scratch,
            affine_scratch,
            square_scratch,
            square_scratch,
            project_scratch,
        ],
        compiler_params=params,
    )(
        place,
        returned,
        pair_map,
        normed,
        norm_gain,
        norm_bias,
        out_weight,
        gate_weight,
        proj_weight,
    )
    returned = exchange(triangle(exchange(send), True))

    return pl.pallas_call(
        leave_kernel,
        out_shape=jax.ShapeDtypeStruct(state_shape, jnp.float32),
        in_specs=[vmem] * 7,
        out_specs=outside,
        scratch_shapes=[
            pltpu.VMEM(state_shape, jnp.float32),
            copies,
            product_scratch,
            stat_scratch,
            affine_scratch,
            square_scratch,
            square_scratch,
        ],
        compiler_params=params,
    )(returned, state, next_normed, norm_gain, norm_bias, out_weight, gate_weight)


def solution(mesh):
    placed = (P("row", "col", None), P(), P(), P(), P(), P(), P())
    return jax.shard_map(
        per_device, mesh=mesh, in_specs=placed, out_specs=P("row", "col", None), check_vma=False
    )
```

```python
import functools

import jax
import jax.numpy as jnp
from jax import lax
from jax.experimental import pallas as pl
from jax.experimental.pallas import tpu as pltpu
from jax.sharding import PartitionSpec as P

epsilon = 1e-05
block_rows = 16
pairs_per_block = block_rows // 2
copy_rows = 4
triangle_parts = 4
fetch_parts = 4
spaced = 18
mesh_axes = ("row", "col")
vmem_bytes = 20 * 1024 * 1024
fetch_vmem_bytes = 48 * 1024 * 1024


def standardise(values):
    count = values.shape[0]
    centre = jnp.sum(values, axis=0, keepdims=True) * (1.0 / count)
    centred = values - centre
    variance = jnp.sum(centred * centred, axis=0, keepdims=True) * (1.0 / count)
    return centred * lax.rsqrt(variance + epsilon)


def norm_over_channels(values, gain, offset):
    return standardise(values) * gain + offset


def turn_weights(layer, place_in, place_out):
    channels = place_in.shape[1]
    if len(place_in.shape) == 4:
        raw = place_in[layer].astype(jnp.float32) * 0.5
        for g in range(place_in.shape[2]):
            place_out[g * channels : (g + 1) * channels, :] = raw[:, g, :].T.astype(jnp.bfloat16)
    else:
        place_out[...] = (place_in[layer].astype(jnp.float32) * 0.5).T.astype(jnp.bfloat16)


def turn_affine(layer, which, gain_ref, bias_ref, affine_ref):
    channels, cols = affine_ref.shape[1:]
    for at, ref in enumerate((gain_ref, bias_ref)):
        line = ref[layer, which : which + 1, :]
        affine_ref[at] = jnp.broadcast_to(line, (cols, channels)).T


def block_pair(row):
    return row // block_rows, row % block_rows


def project_pair(row, place_ref, normed_ref, weight_ref, factor_scratch):
    channels, cols = normed_ref.shape[1:]
    limit, row_base, col_base = place_ref[0], place_ref[1], place_ref[2]
    col_pos = col_base + lax.broadcasted_iota(jnp.int32, (1, cols), 1)
    block, at = block_pair(row)
    kept = []
    for t in range(2):
        keep = jnp.logical_and(col_pos < limit, row_base + row + t < limit)
        kept.append(normed_ref[row + t] * keep.astype(jnp.float32).astype(jnp.bfloat16))
    for side in range(2):
        for t in range(2):
            both = jnp.dot(
                weight_ref[2 * side * channels : 2 * (side + 1) * channels, :],
                kept[t],
                preferred_element_type=jnp.float32,
            )
            factor = (jnp.tanh(both[channels:]) + 1.0) * both[:channels]
            first = side * channels * spaced + at + t
            factor_scratch[block % 2, pl.ds(first, channels, stride=spaced), :] = factor


def write_part(block, part, factor_scratch, send_ref):
    channels = send_ref.shape[0]
    some = channels // pairs_per_block
    for side in range(2):
        first = (side * channels + part * some) * spaced
        rows = slice(block * block_rows, (block + 1) * block_rows)
        for c in range(some):
            at = first + c * spaced
            values = factor_scratch[block % 2, at : at + block_rows, :]
            send_ref[part * some + c, side, rows, :] = values.astype(send_ref.dtype)


def sum_part(block, part, sums, returned_ref, product_scratch):
    channels = returned_ref.shape[0]
    some = channels // pairs_per_block
    rows = slice(block * block_rows, (block + 1) * block_rows)
    first = returned_ref[0, rows, :].astype(jnp.float32)
    total, squares = sums
    for c in range(part * some, (part + 1) * some):
        values = returned_ref[c, rows, :].astype(jnp.float32)
        product_scratch[block % 2, c * spaced : c * spaced + block_rows, :] = values
        shifted = values - first
        total = total + shifted
        squares = squares + shifted * shifted
    return total, squares


def finish_sums(block, sums, returned_ref, stat_scratch):
    channels = returned_ref.shape[0]
    rows = slice(block * block_rows, (block + 1) * block_rows)
    shift = sums[0] * (1.0 / channels)
    variance = sums[1] * (1.0 / channels) - shift * shift
    stat_scratch[block % 2, 0] = returned_ref[0, rows, :].astype(jnp.float32) + shift
    stat_scratch[block % 2, 1] = lax.rsqrt(jnp.maximum(variance, 0.0) + epsilon)


def update_pair(row, normed_ref, affine_ref, out_ref, gate_ref, product_scratch, stat_scratch):
    channels = normed_ref.shape[1]
    block, at = block_pair(row)
    hidden = []
    for t in range(2):
        values = product_scratch[block % 2, pl.ds(at + t, channels, stride=spaced), :]
        centre = stat_scratch[block % 2, 0, at + t : at + t + 1, :]
        scale = stat_scratch[block % 2, 1, at + t : at + t + 1, :]
        out = (values - centre) * scale * affine_ref[0] + affine_ref[1]
        hidden.append(out.astype(jnp.bfloat16))
    term = jnp.dot(
        out_ref[...], jnp.concatenate(hidden, axis=1), preferred_element_type=jnp.float32
    )
    normed = jnp.concatenate([normed_ref[row], normed_ref[row + 1]], axis=1)
    gate = jnp.tanh(jnp.dot(gate_ref[...], normed, preferred_element_type=jnp.float32)) + 1.0
    return gate * term


def fetch_kernel(place_ref, state_ref, standard_ref, state_buf, sems):
    n_rows = state_buf.shape[0]
    fetch_rows = n_rows // sems.shape[0]

    def fetch(b):
        rows = pl.ds(b * fetch_rows, fetch_rows)
        return pltpu.make_async_copy(state_ref.at[rows], state_buf.at[rows], sems.at[b])

    for b in range(sems.shape[0]):
        fetch(b).start()
    for row in range(n_rows):
        if row % fetch_rows == 0:
            fetch(row // fetch_rows).wait()
        standard_ref[row] = standardise(state_buf[row].T)


def enter_kernel(
    place_ref,
    standard_ref,
    project_ref,
    gain_ref,
    bias_ref,
    send_ref,
    normed_ref,
    factor_scratch,
    weight_ref,
    affine_ref,
):
    n_rows = standard_ref.shape[0]
    n_pairs = n_rows // 2
    n_blocks = n_rows // block_rows
    turn_weights(0, project_ref, weight_ref)
    turn_affine(0, 0, gain_ref, bias_ref, affine_ref)

    def normalise(pair):
        if pair < n_pairs:
            for row in (2 * pair, 2 * pair + 1):
                out = standard_ref[row] * affine_ref[0] + affine_ref[1]
                normed_ref[row] = out.astype(jnp.bfloat16)

    normalise(0)
    for block in range(n_blocks + 1):
        for part in range(pairs_per_block):
            pair = block * pairs_per_block + part
            normalise(pair + 1)
            if block < n_blocks:
                project_pair(2 * pair, place_ref, normed_ref, weight_ref, factor_scratch)
            if block > 0:
                write_part(block - 1, part, factor_scratch, send_ref)


def middle_kernel(
    place_ref,
    returned_ref,
    state_ref,
    normed_in_ref,
    gain_ref,
    bias_ref,
    out_ref,
    gate_ref,
    project_ref,
    send_ref,
    normed_ref,
    new_state_ref,
    factor_scratch,
    product_scratch,
    stat_scratch,
    affine_ref,
    next_affine_ref,
    out_weight_ref,
    gate_weight_ref,
    next_weight_ref,
):
    n_rows, channels, cols = new_state_ref.shape
    n_pairs = n_rows // 2
    n_blocks = n_rows // block_rows
    turn_affine(0, 1, gain_ref, bias_ref, affine_ref)
    turn_affine(1, 0, gain_ref, bias_ref, next_affine_ref)
    turn_weights(0, out_ref, out_weight_ref)
    turn_weights(0, gate_ref, gate_weight_ref)
    turn_weights(1, project_ref, next_weight_ref)
    nothing = jnp.zeros((block_rows, cols), jnp.float32)

    def update(pair):
        row = 2 * pair
        term = update_pair(
            row,
            normed_in_ref,
            affine_ref,
            out_weight_ref,
            gate_weight_ref,
            product_scratch,
            stat_scratch,
        )
        for t in range(2):
            values = state_ref[row + t].T + term[:, t * cols : (t + 1) * cols]
            new_state_ref[row + t] = values
            out = norm_over_channels(values, next_affine_ref[0], next_affine_ref[1])
            normed_ref[row + t] = out.astype(jnp.bfloat16)

    for block in range(n_blocks + 3):
        sums = (nothing, nothing)
        for part in range(pairs_per_block):
            if block < n_blocks:
                sums = sum_part(block, part, sums, returned_ref, product_scratch)
            pair = (block - 1) * pairs_per_block + part
            if 0 <= pair < n_pairs:
                update(pair)
            if 0 <= pair - 1 < n_pairs:
                project_pair(
                    2 * (pair - 1), place_ref, normed_ref, next_weight_ref, factor_scratch
                )
            written = (block - 2) * pairs_per_block + part - 1
            if 0 <= written < n_pairs:
                write_part(
                    written // pairs_per_block, written % pairs_per_block, factor_scratch, send_ref
                )
        if block < n_blocks:
            finish_sums(block, sums, returned_ref, stat_scratch)


def leave_kernel(
    returned_ref,
    state_ref,
    normed_in_ref,
    gain_ref,
    bias_ref,
    out_ref,
    gate_ref,
    result_ref,
    result_buf,
    sems,
    product_scratch,
    stat_scratch,
    affine_ref,
    out_weight_ref,
    gate_weight_ref,
):
    n_rows, cols, channels = result_buf.shape
    n_blocks = n_rows // block_rows
    store_rows = n_rows // sems.shape[0]
    turn_affine(1, 1, gain_ref, bias_ref, affine_ref)
    turn_weights(1, out_ref, out_weight_ref)
    turn_weights(1, gate_ref, gate_weight_ref)
    nothing = jnp.zeros((block_rows, cols), jnp.float32)

    def store(b):
        rows = pl.ds(b * store_rows, store_rows)
        return pltpu.make_async_copy(result_buf.at[rows], result_ref.at[rows], sems.at[b])

    for block in range(n_blocks + 1):
        sums = (nothing, nothing)
        for part in range(pairs_per_block):
            if block < n_blocks:
                sums = sum_part(block, part, sums, returned_ref, product_scratch)
            row = 2 * ((block - 1) * pairs_per_block + part)
            if row >= 0:
                term = update_pair(
                    row,
                    normed_in_ref,
                    affine_ref,
                    out_weight_ref,
                    gate_weight_ref,
                    product_scratch,
                    stat_scratch,
                )
                for t in range(2):
                    values = state_ref[row + t] + term[:, t * cols : (t + 1) * cols]
                    result_buf[row + t] = values.T
                if (row + 2) % store_rows == 0:
                    store(row // store_rows).start()
        if block < n_blocks:
            finish_sums(block, sums, returned_ref, stat_scratch)
    for b in range(sems.shape[0]):
        store(b).wait()


def triangle_kernel(n_row, n_col, incoming, received_ref, send_ref, left_mat, right_mat):
    tile_rows, tile_cols = received_ref.shape[2:]
    n_parts = left_mat.shape[0]
    part_rows = n_row * tile_rows // n_parts

    def stage(side, r, s, place_ref, row0, col0):
        place_ref[row0 : row0 + tile_rows, col0 : col0 + tile_cols] = received_ref[
            r * n_col + s, side
        ]

    def stage_left(part):
        place_ref = left_mat.at[part]
        if incoming:
            per_part = n_col // n_parts
            for r in range(n_row):
                for s in range(per_part):
                    stage(0, r, part * per_part + s, place_ref, r * tile_rows, s * tile_cols)
        else:
            per_part = n_row // n_parts
            for r in range(per_part):
                for s in range(n_col):
                    stage(0, part * per_part + r, s, place_ref, r * tile_rows, s * tile_cols)

    stage_left(0)
    for r in range(n_row):
        for s in range(n_col):
            stage(1, r, s, right_mat, r * tile_rows, s * tile_cols)
    summed = (((0,), (0,)), ((), ())) if incoming else (((1,), (1,)), ((), ()))
    for part in range(n_parts):
        if part + 1 < n_parts:
            stage_left(part + 1)
        product = lax.dot_general(
            left_mat[part], right_mat[...], summed, preferred_element_type=jnp.float32
        ).astype(send_ref.dtype)
        for r in range(part_rows // tile_rows):
            for s in range(n_col):
                send_ref[(part * (part_rows // tile_rows) + r) * n_col + s] = product[
                    r * tile_rows : (r + 1) * tile_rows, s * tile_cols : (s + 1) * tile_cols
                ]


def per_device(pair_map, valid_length, norm_gain, norm_bias, proj_weight, gate_weight, out_weight):
    tile_rows, tile_cols, channels = pair_map.shape
    n_row = lax.axis_size("row")
    n_col = lax.axis_size("col")
    n_dev = n_row * n_col
    place = jnp.concatenate(
        [
            valid_length,
            jnp.stack([lax.axis_index("row") * tile_rows, lax.axis_index("col") * tile_cols]),
        ]
    ).astype(jnp.int32)
    params = pltpu.CompilerParams(vmem_limit_bytes=vmem_bytes)
    smem = pl.BlockSpec(memory_space=pltpu.SMEM)
    vmem = pl.BlockSpec(memory_space=pltpu.VMEM)
    outside = pl.BlockSpec(memory_space=pltpu.HBM)
    send_shape = jax.ShapeDtypeStruct((channels, 2, tile_rows, tile_cols), jnp.bfloat16)
    normed_shape = jax.ShapeDtypeStruct((tile_rows, channels, tile_cols), jnp.bfloat16)
    turned_shape = jax.ShapeDtypeStruct((tile_rows, channels, tile_cols), jnp.float32)
    state_shape = (tile_rows, tile_cols, channels)
    factor_scratch = pltpu.VMEM((2, (2 * channels + 1) * spaced, tile_cols), jnp.float32)
    product_scratch = pltpu.VMEM((2, (channels + 1) * spaced, tile_cols), jnp.float32)
    stat_scratch = pltpu.VMEM((2, 2, block_rows, tile_cols), jnp.float32)
    affine_scratch = pltpu.VMEM((2, channels, tile_cols), jnp.float32)
    square_scratch = pltpu.VMEM((channels, channels), jnp.bfloat16)
    project_scratch = pltpu.VMEM((4 * channels, channels), jnp.bfloat16)
    copies = pltpu.SemaphoreType.DMA((tile_rows // copy_rows,))

    def exchange(blocks):
        return lax.all_to_all(blocks, mesh_axes, 0, 0, tiled=True)

    def triangle(received, incoming):
        tokens = n_row * tile_rows
        part = tokens // triangle_parts
        left_shape = (tokens, part) if incoming else (part, tokens)
        return pl.pallas_call(
            functools.partial(triangle_kernel, n_row, n_col, incoming),
            out_shape=jax.ShapeDtypeStruct((n_dev, tile_rows, tile_cols), jnp.bfloat16),
            in_specs=[vmem],
            out_specs=vmem,
            scratch_shapes=[
                pltpu.VMEM((triangle_parts,) + left_shape, jnp.bfloat16),
                pltpu.VMEM((tokens, tokens), jnp.bfloat16),
            ],
            compiler_params=params,
        )(received)

    standard = pl.pallas_call(
        fetch_kernel,
        out_shape=turned_shape,
        in_specs=[smem, outside],
        out_specs=vmem,
        scratch_shapes=[
            pltpu.VMEM(state_shape, jnp.float32),
            pltpu.SemaphoreType.DMA((fetch_parts,)),
        ],
        compiler_params=pltpu.CompilerParams(vmem_limit_bytes=fetch_vmem_bytes),
    )(place, pair_map)
    send, normed = pl.pallas_call(
        enter_kernel,
        out_shape=[send_shape, normed_shape],
        in_specs=[smem, vmem, vmem, vmem, vmem],
        out_specs=[vmem, vmem],
        scratch_shapes=[factor_scratch, project_scratch, affine_scratch],
        compiler_params=params,
    )(place, standard, proj_weight, norm_gain, norm_bias)
    returned = exchange(triangle(exchange(send), False))

    send, next_normed, state = pl.pallas_call(
        middle_kernel,
        out_shape=[send_shape, normed_shape, turned_shape],
        in_specs=[smem] + [vmem] * 8,
        out_specs=[vmem, vmem, vmem],
        scratch_shapes=[
            factor_scratch,
            product_scratch,
            stat_scratch,
            affine_scratch,
            affine_scratch,
            square_scratch,
            square_scratch,
            project_scratch,
        ],
        compiler_params=params,
    )(
        place,
        returned,
        pair_map,
        normed,
        norm_gain,
        norm_bias,
        out_weight,
        gate_weight,
        proj_weight,
    )
    returned = exchange(triangle(exchange(send), True))

    return pl.pallas_call(
        leave_kernel,
        out_shape=jax.ShapeDtypeStruct(state_shape, jnp.float32),
        in_specs=[vmem] * 7,
        out_specs=outside,
        scratch_shapes=[
            pltpu.VMEM(state_shape, jnp.float32),
            copies,
            product_scratch,
            stat_scratch,
            affine_scratch,
            square_scratch,
            square_scratch,
        ],
        compiler_params=params,
    )(returned, state, next_normed, norm_gain, norm_bias, out_weight, gate_weight)


def solution(mesh):
    placed = (P("row", "col", None), P(), P(), P(), P(), P(), P())
    return jax.shard_map(
        per_device, mesh=mesh, in_specs=placed, out_specs=P("row", "col", None), check_vma=False
    )
```

```python
import functools

import jax
import jax.numpy as jnp
from jax import lax
from jax.experimental import pallas as pl
from jax.experimental.pallas import tpu as pltpu
from jax.sharding import PartitionSpec as P

epsilon = 1e-05
block_rows = 16
pairs_per_block = block_rows // 2
copy_rows = 4
triangle_parts = 4
fetch_parts = 4
spaced = 18
mesh_axes = ("row", "col")
vmem_bytes = 20 * 1024 * 1024
fetch_vmem_bytes = 48 * 1024 * 1024


def standardise(values):
    count = values.shape[0]
    centre = jnp.sum(values, axis=0, keepdims=True) * (1.0 / count)
    centred = values - centre
    variance = jnp.sum(centred * centred, axis=0, keepdims=True) * (1.0 / count)
    return centred * lax.rsqrt(variance + epsilon)


def norm_over_channels(values, gain, offset):
    return standardise(values) * gain + offset


def turn_weights(layer, place_in, place_out):
    channels = place_in.shape[1]
    if len(place_in.shape) == 4:
        raw = place_in[layer].astype(jnp.float32) * 0.5
        for g in range(place_in.shape[2]):
            place_out[g * channels : (g + 1) * channels, :] = raw[:, g, :].T.astype(jnp.bfloat16)
    else:
        place_out[...] = (place_in[layer].astype(jnp.float32) * 0.5).T.astype(jnp.bfloat16)


def turn_affine(layer, which, gain_ref, bias_ref, affine_ref):
    channels, cols = affine_ref.shape[1:]
    for at, ref in enumerate((gain_ref, bias_ref)):
        line = ref[layer, which : which + 1, :]
        affine_ref[at] = jnp.broadcast_to(line, (cols, channels)).T


def block_pair(row):
    return row // block_rows, row % block_rows


def project_pair(row, place_ref, normed_ref, weight_ref, factor_scratch):
    channels, cols = normed_ref.shape[1:]
    limit, row_base, col_base = place_ref[0], place_ref[1], place_ref[2]
    col_pos = col_base + lax.broadcasted_iota(jnp.int32, (1, cols), 1)
    block, at = block_pair(row)
    kept = []
    for t in range(2):
        keep = jnp.logical_and(col_pos < limit, row_base + row + t < limit)
        kept.append(normed_ref[row + t] * keep.astype(jnp.float32).astype(jnp.bfloat16))
    for side in range(2):
        for t in range(2):
            both = jnp.dot(
                weight_ref[2 * side * channels : 2 * (side + 1) * channels, :],
                kept[t],
                preferred_element_type=jnp.float32,
            )
            factor = (jnp.tanh(both[channels:]) + 1.0) * both[:channels]
            first = side * channels * spaced + at + t
            factor_scratch[block % 2, pl.ds(first, channels, stride=spaced), :] = factor


def write_part(block, part, factor_scratch, send_ref):
    channels = send_ref.shape[0]
    some = channels // pairs_per_block
    for side in range(2):
        first = (side * channels + part * some) * spaced
        rows = slice(block * block_rows, (block + 1) * block_rows)
        for c in range(some):
            at = first + c * spaced
            values = factor_scratch[block % 2, at : at + block_rows, :]
            send_ref[part * some + c, side, rows, :] = values.astype(send_ref.dtype)


def sum_part(block, part, sums, returned_ref, product_scratch):
    channels = returned_ref.shape[0]
    some = channels // pairs_per_block
    rows = slice(block * block_rows, (block + 1) * block_rows)
    first = returned_ref[0, rows, :].astype(jnp.float32)
    total, squares = sums
    for c in range(part * some, (part + 1) * some):
        values = returned_ref[c, rows, :].astype(jnp.float32)
        product_scratch[block % 2, c * spaced : c * spaced + block_rows, :] = values
        shifted = values - first
        total = total + shifted
        squares = squares + shifted * shifted
    return total, squares


def finish_sums(block, sums, returned_ref, stat_scratch):
    channels = returned_ref.shape[0]
    rows = slice(block * block_rows, (block + 1) * block_rows)
    shift = sums[0] * (1.0 / channels)
    variance = sums[1] * (1.0 / channels) - shift * shift
    stat_scratch[block % 2, 0] = returned_ref[0, rows, :].astype(jnp.float32) + shift
    stat_scratch[block % 2, 1] = lax.rsqrt(jnp.maximum(variance, 0.0) + epsilon)


def update_pair(
    row, normed_ref, affine_ref, out_ref, gate_ref, product_scratch, stat_scratch, folded=False
):
    channels = normed_ref.shape[1]
    block, at = block_pair(row)
    hidden = []
    for t in range(2):
        values = product_scratch[block % 2, pl.ds(at + t, channels, stride=spaced), :]
        centre = stat_scratch[block % 2, 0, at + t : at + t + 1, :]
        scale = stat_scratch[block % 2, 1, at + t : at + t + 1, :]
        out = (values - centre) * scale
        if not folded:
            out = out * affine_ref[0] + affine_ref[1]
        hidden.append(out.astype(jnp.bfloat16))
    term = jnp.dot(
        out_ref[...], jnp.concatenate(hidden, axis=1), preferred_element_type=jnp.float32
    )
    normed = jnp.concatenate([normed_ref[row], normed_ref[row + 1]], axis=1)
    gate = jnp.tanh(jnp.dot(gate_ref[...], normed, preferred_element_type=jnp.float32)) + 1.0
    if folded:
        term = term + jnp.concatenate([affine_ref[1], affine_ref[1]], axis=1)
    return gate * term


def fold_affine(layer, place_in, affine_ref, place_out):
    raw = place_in[layer].astype(jnp.float32) * 0.5
    place_out[...] = (raw * affine_ref[0]).T.astype(jnp.bfloat16)
    constant = jnp.sum(raw * affine_ref[1], axis=0, keepdims=True)
    affine_ref[1] = jnp.broadcast_to(constant, raw.shape).T


def fetch_kernel(place_ref, state_ref, standard_ref, state_buf, sems):
    n_rows = state_buf.shape[0]
    fetch_rows = n_rows // sems.shape[0]

    def fetch(b):
        rows = pl.ds(b * fetch_rows, fetch_rows)
        return pltpu.make_async_copy(state_ref.at[rows], state_buf.at[rows], sems.at[b])

    for b in range(sems.shape[0]):
        fetch(b).start()
    for row in range(n_rows):
        if row % fetch_rows == 0:
            fetch(row // fetch_rows).wait()
        standard_ref[row] = standardise(state_buf[row].T)


def enter_kernel(
    place_ref,
    standard_ref,
    project_ref,
    gain_ref,
    bias_ref,
    send_ref,
    normed_ref,
    factor_scratch,
    weight_ref,
    affine_ref,
):
    n_rows = standard_ref.shape[0]
    n_pairs = n_rows // 2
    n_blocks = n_rows // block_rows
    turn_weights(0, project_ref, weight_ref)
    turn_affine(0, 0, gain_ref, bias_ref, affine_ref)

    def normalise(pair):
        if pair < n_pairs:
            for row in (2 * pair, 2 * pair + 1):
                out = standard_ref[row] * affine_ref[0] + affine_ref[1]
                normed_ref[row] = out.astype(jnp.bfloat16)

    normalise(0)
    for block in range(n_blocks + 1):
        for part in range(pairs_per_block):
            pair = block * pairs_per_block + part
            normalise(pair + 1)
            if block < n_blocks:
                project_pair(2 * pair, place_ref, normed_ref, weight_ref, factor_scratch)
            if block > 0:
                write_part(block - 1, part, factor_scratch, send_ref)


def middle_kernel(
    place_ref,
    returned_ref,
    state_ref,
    normed_in_ref,
    gain_ref,
    bias_ref,
    out_ref,
    gate_ref,
    project_ref,
    send_ref,
    normed_ref,
    new_state_ref,
    factor_scratch,
    product_scratch,
    stat_scratch,
    affine_ref,
    next_affine_ref,
    out_weight_ref,
    gate_weight_ref,
    next_weight_ref,
):
    n_rows, channels, cols = new_state_ref.shape
    n_pairs = n_rows // 2
    n_blocks = n_rows // block_rows
    turn_affine(0, 1, gain_ref, bias_ref, affine_ref)
    turn_affine(1, 0, gain_ref, bias_ref, next_affine_ref)
    turn_weights(0, out_ref, out_weight_ref)
    turn_weights(0, gate_ref, gate_weight_ref)
    turn_weights(1, project_ref, next_weight_ref)
    nothing = jnp.zeros((block_rows, cols), jnp.float32)

    def update(pair):
        row = 2 * pair
        term = update_pair(
            row,
            normed_in_ref,
            affine_ref,
            out_weight_ref,
            gate_weight_ref,
            product_scratch,
            stat_scratch,
        )
        for t in range(2):
            values = state_ref[row + t].T + term[:, t * cols : (t + 1) * cols]
            new_state_ref[row + t] = values
            out = norm_over_channels(values, next_affine_ref[0], next_affine_ref[1])
            normed_ref[row + t] = out.astype(jnp.bfloat16)

    for block in range(n_blocks + 3):
        sums = (nothing, nothing)
        for part in range(pairs_per_block):
            if block < n_blocks:
                sums = sum_part(block, part, sums, returned_ref, product_scratch)
            pair = (block - 1) * pairs_per_block + part
            if 0 <= pair < n_pairs:
                update(pair)
            if 0 <= pair - 1 < n_pairs:
                project_pair(
                    2 * (pair - 1), place_ref, normed_ref, next_weight_ref, factor_scratch
                )
            written = (block - 2) * pairs_per_block + part - 1
            if 0 <= written < n_pairs:
                write_part(
                    written // pairs_per_block, written % pairs_per_block, factor_scratch, send_ref
                )
        if block < n_blocks:
            finish_sums(block, sums, returned_ref, stat_scratch)


def leave_kernel(
    returned_ref,
    state_ref,
    normed_in_ref,
    gain_ref,
    bias_ref,
    out_ref,
    gate_ref,
    result_ref,
    result_buf,
    sems,
    product_scratch,
    stat_scratch,
    affine_ref,
    out_weight_ref,
    gate_weight_ref,
):
    n_rows, cols, channels = result_buf.shape
    n_blocks = n_rows // block_rows
    store_rows = n_rows // sems.shape[0]
    turn_affine(1, 1, gain_ref, bias_ref, affine_ref)
    fold_affine(1, out_ref, affine_ref, out_weight_ref)
    turn_weights(1, gate_ref, gate_weight_ref)
    nothing = jnp.zeros((block_rows, cols), jnp.float32)

    def store(b):
        rows = pl.ds(b * store_rows, store_rows)
        return pltpu.make_async_copy(result_buf.at[rows], result_ref.at[rows], sems.at[b])

    for block in range(n_blocks + 1):
        sums = (nothing, nothing)
        for part in range(pairs_per_block):
            if block < n_blocks:
                sums = sum_part(block, part, sums, returned_ref, product_scratch)
            row = 2 * ((block - 1) * pairs_per_block + part)
            if row >= 0:
                term = update_pair(
                    row,
                    normed_in_ref,
                    affine_ref,
                    out_weight_ref,
                    gate_weight_ref,
                    product_scratch,
                    stat_scratch,
                    folded=True,
                )
                for t in range(2):
                    values = state_ref[row + t] + term[:, t * cols : (t + 1) * cols]
                    result_buf[row + t] = values.T
                if (row + 2) % store_rows == 0:
                    store(row // store_rows).start()
        if block < n_blocks:
            finish_sums(block, sums, returned_ref, stat_scratch)
    for b in range(sems.shape[0]):
        store(b).wait()


def triangle_kernel(n_row, n_col, incoming, received_ref, send_ref, left_mat, right_mat):
    tile_rows, tile_cols = received_ref.shape[2:]
    n_parts = left_mat.shape[0]
    part_rows = n_row * tile_rows // n_parts

    def stage(side, r, s, place_ref, row0, col0):
        place_ref[row0 : row0 + tile_rows, col0 : col0 + tile_cols] = received_ref[
            r * n_col + s, side
        ]

    def stage_left(part):
        place_ref = left_mat.at[part]
        if incoming:
            per_part = n_col // n_parts
            for r in range(n_row):
                for s in range(per_part):
                    stage(0, r, part * per_part + s, place_ref, r * tile_rows, s * tile_cols)
        else:
            per_part = n_row // n_parts
            for r in range(per_part):
                for s in range(n_col):
                    stage(0, part * per_part + r, s, place_ref, r * tile_rows, s * tile_cols)

    stage_left(0)
    for r in range(n_row):
        for s in range(n_col):
            stage(1, r, s, right_mat, r * tile_rows, s * tile_cols)
    summed = (((0,), (0,)), ((), ())) if incoming else (((1,), (1,)), ((), ()))
    for part in range(n_parts):
        if part + 1 < n_parts:
            stage_left(part + 1)
        product = lax.dot_general(
            left_mat[part], right_mat[...], summed, preferred_element_type=jnp.float32
        ).astype(send_ref.dtype)
        for r in range(part_rows // tile_rows):
            for s in range(n_col):
                send_ref[(part * (part_rows // tile_rows) + r) * n_col + s] = product[
                    r * tile_rows : (r + 1) * tile_rows, s * tile_cols : (s + 1) * tile_cols
                ]


def per_device(pair_map, valid_length, norm_gain, norm_bias, proj_weight, gate_weight, out_weight):
    tile_rows, tile_cols, channels = pair_map.shape
    n_row = lax.axis_size("row")
    n_col = lax.axis_size("col")
    n_dev = n_row * n_col
    place = jnp.concatenate(
        [
            valid_length,
            jnp.stack([lax.axis_index("row") * tile_rows, lax.axis_index("col") * tile_cols]),
        ]
    ).astype(jnp.int32)
    params = pltpu.CompilerParams(vmem_limit_bytes=vmem_bytes)
    smem = pl.BlockSpec(memory_space=pltpu.SMEM)
    vmem = pl.BlockSpec(memory_space=pltpu.VMEM)
    outside = pl.BlockSpec(memory_space=pltpu.HBM)
    send_shape = jax.ShapeDtypeStruct((channels, 2, tile_rows, tile_cols), jnp.bfloat16)
    normed_shape = jax.ShapeDtypeStruct((tile_rows, channels, tile_cols), jnp.bfloat16)
    turned_shape = jax.ShapeDtypeStruct((tile_rows, channels, tile_cols), jnp.float32)
    state_shape = (tile_rows, tile_cols, channels)
    factor_scratch = pltpu.VMEM((2, (2 * channels + 1) * spaced, tile_cols), jnp.float32)
    product_scratch = pltpu.VMEM((2, (channels + 1) * spaced, tile_cols), jnp.float32)
    stat_scratch = pltpu.VMEM((2, 2, block_rows, tile_cols), jnp.float32)
    affine_scratch = pltpu.VMEM((2, channels, tile_cols), jnp.float32)
    square_scratch = pltpu.VMEM((channels, channels), jnp.bfloat16)
    project_scratch = pltpu.VMEM((4 * channels, channels), jnp.bfloat16)
    copies = pltpu.SemaphoreType.DMA((tile_rows // copy_rows,))

    def exchange(blocks):
        return lax.all_to_all(blocks, mesh_axes, 0, 0, tiled=True)

    def triangle(received, incoming):
        tokens = n_row * tile_rows
        part = tokens // triangle_parts
        left_shape = (tokens, part) if incoming else (part, tokens)
        return pl.pallas_call(
            functools.partial(triangle_kernel, n_row, n_col, incoming),
            out_shape=jax.ShapeDtypeStruct((n_dev, tile_rows, tile_cols), jnp.bfloat16),
            in_specs=[vmem],
            out_specs=vmem,
            scratch_shapes=[
                pltpu.VMEM((triangle_parts,) + left_shape, jnp.bfloat16),
                pltpu.VMEM((tokens, tokens), jnp.bfloat16),
            ],
            compiler_params=params,
        )(received)

    standard = pl.pallas_call(
        fetch_kernel,
        out_shape=turned_shape,
        in_specs=[smem, outside],
        out_specs=vmem,
        scratch_shapes=[
            pltpu.VMEM(state_shape, jnp.float32),
            pltpu.SemaphoreType.DMA((fetch_parts,)),
        ],
        compiler_params=pltpu.CompilerParams(vmem_limit_bytes=fetch_vmem_bytes),
    )(place, pair_map)
    send, normed = pl.pallas_call(
        enter_kernel,
        out_shape=[send_shape, normed_shape],
        in_specs=[smem, vmem, vmem, vmem, vmem],
        out_specs=[vmem, vmem],
        scratch_shapes=[factor_scratch, project_scratch, affine_scratch],
        compiler_params=params,
    )(place, standard, proj_weight, norm_gain, norm_bias)
    returned = exchange(triangle(exchange(send), False))

    send, next_normed, state = pl.pallas_call(
        middle_kernel,
        out_shape=[send_shape, normed_shape, turned_shape],
        in_specs=[smem] + [vmem] * 8,
        out_specs=[vmem, vmem, vmem],
        scratch_shapes=[
            factor_scratch,
            product_scratch,
            stat_scratch,
            affine_scratch,
            affine_scratch,
            square_scratch,
            square_scratch,
            project_scratch,
        ],
        compiler_params=params,
    )(
        place,
        returned,
        pair_map,
        normed,
        norm_gain,
        norm_bias,
        out_weight,
        gate_weight,
        proj_weight,
    )
    returned = exchange(triangle(exchange(send), True))

    return pl.pallas_call(
        leave_kernel,
        out_shape=jax.ShapeDtypeStruct(state_shape, jnp.float32),
        in_specs=[vmem] * 7,
        out_specs=outside,
        scratch_shapes=[
            pltpu.VMEM(state_shape, jnp.float32),
            copies,
            product_scratch,
            stat_scratch,
            affine_scratch,
            square_scratch,
            square_scratch,
        ],
        compiler_params=params,
    )(returned, state, next_normed, norm_gain, norm_bias, out_weight, gate_weight)


def solution(mesh):
    placed = (P("row", "col", None), P(), P(), P(), P(), P(), P())
    return jax.shard_map(
        per_device, mesh=mesh, in_specs=placed, out_specs=P("row", "col", None), check_vma=False
    )
```
